512 devices in a mesh: seq: 32 (over x, y), head: 16 (over z, core).
Axes of the slice: x: 4, y: 8, z: 8, core: 2. Of those that a mesh axis runs over, the one named last changes fastest.
Arguments:
- queries: bfloat16 [114688, 2048], P(('seq', 'head')), may hold values from -110 to 110
- key_rows: bfloat16 [114688, 2048], P(('seq', 'head')), may hold values from -6 to 6
- value_rows: bfloat16 [114688, 2048], P(('seq', 'head')), may hold values from -6 to 6
- token_rank: int32 [32, 3584], P('seq'), may hold values from 0 to 3583, each once within a row
- masked_index: int32 [32, 224], P('seq'), may hold values from 0 to 3583, as said below
- masked_counts: int32 [32], replicated, may hold values from 1 to 224, 2368 in all
- clean_latents: bfloat16 [114688, 16], P('seq'), may hold values from -6 to 6
- noise_draws: bfloat16 [114688, 64], P('seq'), may hold values from -6 to 6
- noise_times: bfloat16 [114688, 4], P('seq'), may hold values from 0.049804688 to 0.94921875
- w_cond: bfloat16 [2048, 1536], P('head'), may hold values from -0.5 to 0.5
- w_in: float32 [16, 1536], replicated, may hold values from -1.5 to 1.5
- time_vec: float32 [1536], replicated, may hold values from -5 to 5
- norm_gain: float32 [1536], replicated, may hold values from 0.25 to 1.75
- w_out: float32 [1536, 16], replicated, may hold values from -0.15625 to 0.15625
Outputs:
- attended: bfloat16 [114688, 2048], P(('seq', 'head'))
- grad_cond: float32 [2048, 1536], P('head')
- grad_in: float32 [16, 1536], replicated
- grad_time: float32 [1536], replicated
- grad_gain: float32 [1536], replicated
- grad_out: float32 [1536, 16], replicated
The draws below stay inside these ranges and needn't reach their ends.
Inputs may be any that keep to these rules, and one draw needn't show every extreme that they name: `token_rank`: each clip's row holds each rank once. `masked_index`: row s holds 224 distinct positions within clip s; only its first masked_counts[s] entries are used. `masked_counts`: they sum to 2368; the largest is 224.
All inputs are finite; a program needn't handle non-finite values.
Results may differ from the reference program's by a relative error of at most 0.009.
Values may be sent and summed in bfloat16 or wider, within the bound.
No kernel may reach another device: no remote copies, remote signals or barrier semaphores. Data moves between devices by JAX's collectives and lax.ppermute only.
A program may use at most 64 MiB of HBM per device.

```python
import math
import jax
import jax.numpy as jnp
import numpy as np
from jax import lax

HD = 128
HEADS = 16
WIDTH = 1536
LAT = 16
DRAWS = 4
SEQ_DEV = 3584
TOKENS = 114688
MOST = 224
MASKED = 2368
N_SEQ = 32


def pair_fields(key):
    keys_float = jnp.clip(jax.random.normal(jax.random.fold_in(key, 11), (TOKENS, HEADS * HD), jnp.float32), -6.0, 6.0)
    query_float = jnp.clip(jax.random.normal(jax.random.fold_in(key, 12), (TOKENS, HEADS * HD), jnp.float32), -6.0, 6.0)
    return (query_float, keys_float)


def draw_queries(key, part):
    query_float, keys_float = pair_fields(key)
    return query_float.astype(jnp.bfloat16)


def draw_key_rows(key, part):
    query_float, keys_float = pair_fields(key)
    return keys_float.astype(jnp.bfloat16)


def draw_masked_index(key, part):
    key = jax.random.fold_in(key, 3)
    row_keys = jax.random.split(key, N_SEQ)
    chosen = jax.vmap(lambda row_key: jax.random.permutation(row_key, SEQ_DEV)[:MOST])(row_keys)
    return chosen.astype(jnp.int32)


def levels(own_key, extent, cuts, low, top_value):
    gain, own = 1.0, jax.random.fold_in(own_key, 6)
    for dim, shards_of in cuts:
        steps = jnp.exp(jax.random.uniform(jax.random.fold_in(own, dim), (shards_of,), jnp.float32, low / len(cuts), top_value / len(cuts)))
        gain = gain * jnp.repeat(steps, extent[dim] // shards_of).reshape([-1 if axis == dim else 1 for axis in range(len(extent))])
    return gain


def split_up(count, total, limit, lean):
    portions = [(1 << 20) // math.isqrt(rank ** lean) + 1 for rank in range(2, count + 1)]
    rest, holding = total - limit - (count - 1), [1] * (count - 1)
    while rest > 0:
        free = [i for i in range(count - 1) if holding[i] < limit]
        whole, remaining = sum([portions[i] for i in free]), rest
        for i in free:
            addition = min(limit - holding[i], max(1, remaining * portions[i] // whole), rest)
            holding[i] = holding[i] + addition
            rest = rest - addition
    return np.array([limit] + holding)


def uneven(key, amount, total, reach, lean):
    if amount == 2:
        one = jax.random.randint(key, (), max(1, total - reach), min(reach, total - 1) + 1)
        return jnp.stack([one, total - one])
    tallies = jnp.asarray(split_up(amount, total, reach, lean), jnp.int32)
    twos = (amount - 1) // 2
    giver, taker = tallies[1:1 + 2 * twos:2], tallies[2:2 + 2 * twos:2]
    slack = jnp.minimum(giver - 1, reach - taker)
    shifted = jax.random.randint(jax.random.fold_in(key, 1), (twos,), 0, 1 << 20) % (slack + 1)
    tallies = tallies.at[1:1 + 2 * twos:2].set(giver - shifted).at[2:2 + 2 * twos:2].set(taker + shifted)
    return tallies[jax.random.permutation(jax.random.fold_in(key, 2), amount)]


def scatter_about(own_key, extent, scale, most, shards=(), held_as=jnp.bfloat16):
    factor_of = levels(own_key, extent, shards, -0.22, 0.18) if shards else 1.0
    drawn = jax.random.normal(own_key, extent, jnp.float32) * scale * factor_of
    return jnp.minimum(jnp.maximum(drawn, -most), most).astype(held_as)


def setup_inputs(seed: int = 0) -> dict:
    key_of = jax.random.split(jax.random.key(seed), 15)
    queries = draw_queries(jax.random.fold_in(key_of[14], 71), 0)
    key_rows = draw_key_rows(jax.random.fold_in(key_of[14], 71), 0)
    value_rows = scatter_about(key_of[2], (TOKENS, HEADS * HD), 1.0, 6.0, ((0, 512),))
    token_rank = jax.vmap(lambda own: jax.random.permutation(own, SEQ_DEV))(jax.random.split(key_of[3], N_SEQ)).reshape((N_SEQ, SEQ_DEV)).astype(jnp.int32)
    masked_index = draw_masked_index(jax.random.fold_in(key_of[14], 71), 0)
    masked_counts = uneven(key_of[5], N_SEQ, MASKED, MOST, 2).astype(jnp.int32)
    clean_latents = scatter_about(key_of[6], (TOKENS, LAT), 1.0, 6.0, ((0, 32),))
    noise_draws = scatter_about(key_of[7], (TOKENS, DRAWS * LAT), 1.0, 6.0, ((0, 32),))
    noise_times = jnp.clip(0.049804688 + 0.89941406 * jax.random.uniform(key_of[8], (TOKENS, DRAWS), jnp.float32) ** levels(key_of[8], (TOKENS, DRAWS), ((0, 32),), -0.2, 0.2), 0.049804688, 0.94921875).astype(jnp.bfloat16)
    w_cond = scatter_about(key_of[9], (HEADS * HD, WIDTH), HD ** -0.5, 0.5, ((0, 16),))
    w_in = scatter_about(key_of[10], (LAT, WIDTH), LAT ** -0.5, 1.5, (), jnp.float32)
    time_vec = scatter_about(key_of[11], (WIDTH,), 1.0, 5.0, (), jnp.float32)
    norm_gain = jnp.clip(1.0 + 0.15 * jax.random.normal(key_of[12], (WIDTH,), jnp.float32), 0.25, 1.75)
    w_out = scatter_about(key_of[13], (WIDTH, LAT), WIDTH ** -0.5, 0.15625, (), jnp.float32)
    return {"queries": queries, "key_rows": key_rows, "value_rows": value_rows, "token_rank": token_rank, "masked_index": masked_index, "masked_counts": masked_counts, "clean_latents": clean_latents, "noise_draws": noise_draws, "noise_times": noise_times, "w_cond": w_cond, "w_in": w_in, "time_vec": time_vec, "norm_gain": norm_gain, "w_out": w_out}


NORM_EPS = 1e-06

def head_loss(condition, w_in, time_vec, norm_gain, w_out, payload, row_weight, loss_scale):
    row_count = condition.shape[0]
    load_float = payload.astype(jnp.float32)
    clean_part = load_float[:, :LAT]
    noise_part = load_float[:, LAT:LAT + DRAWS * LAT].reshape(row_count, DRAWS, LAT)
    time_part = load_float[:, LAT + DRAWS * LAT:]
    angles = 0.5 * math.pi * time_part
    noisy_input = jnp.cos(angles)[:, :, None] * clean_part[:, None, :] + jnp.sin(angles)[:, :, None] * noise_part
    hidden = jnp.einsum('rdc,cw->rdw', noisy_input, w_in, precision=lax.Precision.HIGHEST)
    hidden = hidden + condition[:, None, :] + time_part[:, :, None] * time_vec
    normed = hidden * lax.rsqrt(lax.optimization_barrier(jnp.mean(hidden * hidden, axis=-1, keepdims=True)) + NORM_EPS) * norm_gain
    activated = jax.nn.silu(normed)
    predicted = jnp.einsum('rdw,wc->rdc', activated, w_out, precision=lax.Precision.HIGHEST)
    residual = predicted - noise_part
    return jnp.sum(row_weight[:, None, None] * residual * residual) * loss_scale

def attend_head(head_query, head_key, head_value, clip_rank):
    block_rows = math.gcd(SEQ_DEV, 512)
    factor = 1.0 / math.sqrt(HD)

    def one_block(first_row):
        query_block = lax.dynamic_slice_in_dim(head_query, first_row, block_rows, 0)
        rank_block = lax.dynamic_slice_in_dim(clip_rank, first_row, block_rows, 0)
        scores = jnp.dot(query_block, head_key.T, preferred_element_type=jnp.float32) * factor
        visible = clip_rank[None, :] <= rank_block[:, None]
        row_max = lax.optimization_barrier(jnp.max(jnp.where(visible, scores, -jnp.inf), axis=1, keepdims=True))
        weights = jnp.where(visible, jnp.exp(scores - row_max), 0.0)
        row_sum = lax.optimization_barrier(jnp.sum(weights, axis=1, keepdims=True))
        mixed_block = jnp.dot(weights.astype(jnp.bfloat16), head_value, preferred_element_type=jnp.float32)
        return (mixed_block / row_sum).astype(jnp.bfloat16)
    starts = jnp.arange(SEQ_DEV // block_rows, dtype=jnp.int32) * block_rows
    return lax.map(one_block, starts).reshape(SEQ_DEV, HD)

def reference(queries, key_rows, value_rows, token_rank, masked_index, masked_counts, clean_latents, noise_draws, noise_times, w_cond, w_in, time_vec, norm_gain, w_out):

    def split_heads(matrix):
        shaped = jnp.transpose(matrix.reshape(N_SEQ, SEQ_DEV, HEADS, HD), (0, 2, 1, 3))
        return shaped.reshape(N_SEQ * HEADS, SEQ_DEV, HD)
    rank_rows = jnp.repeat(token_rank.astype(jnp.int32), HEADS, axis=0)

    def per_head(inputs):
        return attend_head(inputs[0], inputs[1], inputs[2], inputs[3])
    per_heads = lax.map(per_head, (split_heads(queries), split_heads(key_rows), split_heads(value_rows), rank_rows))
    attended = jnp.transpose(per_heads.reshape(N_SEQ, HEADS, SEQ_DEV, HD), (0, 2, 1, 3)).reshape(TOKENS, HEADS * HD)
    positions = jnp.arange(N_SEQ, dtype=jnp.int32)[:, None] * SEQ_DEV + masked_index.astype(jnp.int32)
    alive_mask = jnp.arange(MOST, dtype=jnp.int32)[None, :] < masked_counts[:, None]
    payload_all = jnp.concatenate([clean_latents, noise_draws, noise_times], axis=1)
    loss_scale = 1.0 / math.sqrt(MOST // 3 * N_SEQ * DRAWS)

    def one_shard(carry, inputs):
        position_row, alive_row = inputs
        picked_rows = jnp.where(alive_row[:, None], attended[position_row], jnp.zeros((), jnp.bfloat16))
        local_load = payload_all[position_row]
        condition = jnp.dot(picked_rows, w_cond, preferred_element_type=jnp.float32)
        row_weight = jnp.where(alive_row, 1.0, 0.0).astype(condition.dtype)

        def local_loss(cond_in, in_weight, time_weight, gain_weight, out_weight):
            return head_loss(cond_in, in_weight, time_weight, gain_weight, out_weight, local_load, row_weight, loss_scale)
        loss_value, pull_back = jax.vjp(local_loss, condition, w_in, time_vec, norm_gain, w_out)
        cond_grad, in_grad, time_grad, gain_grad, out_grad = pull_back(jnp.ones_like(loss_value))
        cond_part = lax.dot_general(picked_rows, cond_grad.astype(jnp.bfloat16), (((0,), (0,)), ((), ())), preferred_element_type=jnp.float32)
        updated = (carry[0] + cond_part, carry[1] + in_grad, carry[2] + time_grad, carry[3] + gain_grad, carry[4] + out_grad)
        return (updated, None)
    start_state = (jnp.zeros((HEADS * HD, WIDTH), jnp.float32), jnp.zeros((LAT, WIDTH), jnp.float32), jnp.zeros((WIDTH,), jnp.float32), jnp.zeros((WIDTH,), jnp.float32), jnp.zeros((WIDTH, LAT), jnp.float32))
    totals, unused = lax.scan(one_shard, start_state, (positions, alive_mask))
    return (attended, totals[0], totals[1], totals[2], totals[3], totals[4])
```

```python
import functools
import math

import jax
import jax.numpy as jnp
from jax import lax
from jax.experimental import pallas as pl
from jax.experimental.pallas import tpu as pltpu
from jax.sharding import PartitionSpec as P

HD = 128
LAT = 16
DRAWS = 4
NORM_EPS = 1e-06
HIDDEN_SCORE = -1e30
SLOT = 16
EXTRA = 128
PACK = 256
GROUP_ROWS = 16
LOG2E = 1.4426950408889634
F32 = jnp.float32
BF16 = jnp.bfloat16
VMEM_LIMIT = 56 * 1024 * 1024


def params():
    return pltpu.CompilerParams(vmem_limit_bytes=VMEM_LIMIT)


def vmem():
    return pl.BlockSpec(memory_space=pltpu.VMEM)


def anywhere():
    return pl.BlockSpec(memory_space=pl.ANY)


def dot(a, b):
    return jnp.dot(a, b, preferred_element_type=F32)


def two_parts(value):
    high = value.astype(BF16)
    return high, (value - high.astype(F32)).astype(BF16)


def load_keys(k_ref, v_ref, key_scr, val_scr):
    rows = key_scr.shape[0]
    key_scr[...] = k_ref[:, 0].reshape(rows, HD)
    val_scr[:, :HD] = v_ref[:, 0].reshape(rows, HD)
    val_scr[:, HD:] = jnp.ones((rows, HD), BF16)


def attend(query, query_rank, rank_ref, key_scr, val_scr, score_scr):
    total = key_scr.shape[0]
    chunk = math.gcd(total, 512)
    scale = LOG2E / math.sqrt(HD)
    top = None
    for start in range(0, total, chunk):
        scores = lax.dot_general(
            query,
            key_scr[start : start + chunk, :],
            (((1,), (1,)), ((), ())),
            preferred_element_type=F32,
        )
        visible = rank_ref[:, start : start + chunk] <= query_rank
        scores = jnp.where(visible, scores, HIDDEN_SCORE)
        score_scr[:, start : start + chunk] = scores
        for lane in range(0, chunk, 128):
            part = scores[:, lane : lane + 128]
            top = part if top is None else jnp.maximum(top, part)
    top = jnp.max(top, axis=1, keepdims=True)
    total_out = None
    for start in range(0, total, chunk):
        weights = jnp.exp2((score_scr[:, start : start + chunk] - top) * scale)
        mixed = dot(weights.astype(BF16), val_scr[start : start + chunk, :])
        total_out = mixed if total_out is None else total_out + mixed
    return total_out[:, :HD] / total_out[:, HD:]


def masked_kernel(
    q_ref, k_ref, v_ref, where_ref, qrank_ref, rank_ref, w_ref, part_ref, picked_ref,
    key_scr, val_scr, score_scr,
):
    load_keys(k_ref, v_ref, key_scr, val_scr)
    slots = where_ref.shape[0]
    total = key_scr.shape[0]
    chunk = math.gcd(total, 512)
    sources, _, each, _ = q_ref.shape
    query = jnp.zeros((slots, HD), F32)
    step = math.gcd(each * sources, each * 4)
    for start in range(0, total, step):
        lanes = lax.broadcasted_iota(jnp.int32, (slots, step), 1) + start
        hit = jnp.where(lanes == where_ref[...], 1.0, 0.0).astype(BF16)
        rows = q_ref[start // each : (start + step) // each, 0].reshape(step, HD)
        query = query + dot(hit, rows)
    out = attend(query.astype(BF16), qrank_ref[...], rank_ref, key_scr, val_scr, score_scr)
    picked = jnp.where(qrank_ref[...] >= 0, out, 0.0).astype(BF16)
    picked_ref[...] = picked
    part = dot(picked, w_ref[...]).astype(BF16)
    part_ref[...] = part.reshape(part_ref.shape)


def attend_masked(arrived, where, where_rank, rank_row, w_cond):
    heads, _, each, _ = arrived.shape
    total = heads * each
    slots = where.shape[0]
    width = w_cond.shape[1]
    return pl.pallas_call(
        masked_kernel,
        grid=(1,),
        in_specs=[
            pl.BlockSpec((heads, 1, each, HD), lambda i: (0, 0, 0, 0)),
            pl.BlockSpec((heads, 1, each, HD), lambda i: (0, 1, 0, 0)),
            pl.BlockSpec((heads, 1, each, HD), lambda i: (0, 2, 0, 0)),
            vmem(),
            vmem(),
            vmem(),
            vmem(),
        ],
        out_specs=[vmem(), vmem()],
        out_shape=[
            jax.ShapeDtypeStruct((heads, slots // heads, width), BF16),
            jax.ShapeDtypeStruct((slots, HD), BF16),
        ],
        scratch_shapes=[
            pltpu.VMEM((total, HD), BF16),
            pltpu.VMEM((total, 2 * HD), BF16),
            pltpu.VMEM((slots, total), F32),
        ],
        compiler_params=params(),
        name="masked_rows",
    )(arrived, arrived, arrived, where, where_rank, rank_row, w_cond)


def attend_kernel(q_ref, k_ref, v_ref, qrank_ref, rank_ref, *rest):
    out_ref, key_scr, val_scr, score_scr = rest[-4:]

    @pl.when(pl.program_id(0) == 0)
    def _():
        load_keys(k_ref, v_ref, key_scr, val_scr)

    out = attend(q_ref[0, 0], qrank_ref[0], rank_ref, key_scr, val_scr, score_scr)
    out_ref[0] = out.astype(BF16)


def attend_some(arrived, rank_column, rank_row, first, count, after, earlier=None):
    heads, _, each, _ = arrived.shape
    total = heads * each
    specs = [
        pl.BlockSpec((1, 1, each, HD), lambda i: (i + first, 0, 0, 0)),
        pl.BlockSpec((heads, 1, each, HD), lambda i: (0, 1, 0, 0)),
        pl.BlockSpec((heads, 1, each, HD), lambda i: (0, 2, 0, 0)),
        pl.BlockSpec((1, each, 1), lambda i: (i + first, 0, 0)),
        vmem(),
        anywhere(),
    ]
    operands = [arrived, arrived, arrived, rank_column, rank_row, after]
    aliases = {}
    if earlier is not None:
        specs.append(anywhere())
        operands.append(earlier)
        aliases = {len(operands) - 1: 0}
    return pl.pallas_call(
        attend_kernel,
        grid=(count,),
        in_specs=specs,
        out_specs=pl.BlockSpec((1, each, HD), lambda i: (i + first, 0, 0)),
        out_shape=jax.ShapeDtypeStruct((heads, each, HD), BF16),
        scratch_shapes=[
            pltpu.VMEM((total, HD), BF16),
            pltpu.VMEM((total, 2 * HD), BF16),
            pltpu.VMEM((each, total), F32),
        ],
        input_output_aliases=aliases,
        compiler_params=params(),
        name="attention",
    )(*operands)


def head_kernel(
    cond_ref, base_ref, gain_ref, outhi_ref, outlo_ref, outhi_t_ref, outlo_t_ref, noise_ref,
    weight_ref, feat_ref, after_ref, send_ref, block_scr,
):
    heads, rows, width = cond_ref.shape
    count = base_ref.shape[0]
    condition = cond_ref[0].astype(F32)
    for source in range(1, heads):
        condition = condition + cond_ref[source].astype(F32)
    hidden = base_ref[...] + jnp.concatenate([condition] * (count // rows), axis=0)
    inverse = lax.rsqrt(jnp.mean(hidden * hidden, axis=1, keepdims=True) + NORM_EPS)
    unit = hidden * inverse
    gain = gain_ref[...]
    scaled = unit * gain
    gate = 1.0 / (1.0 + jnp.exp(-scaled))
    active = scaled * gate
    act_hi, act_lo = two_parts(active)
    both = dot(jnp.concatenate([act_hi, act_lo], axis=0), outhi_ref[...])
    predicted = both[:count] + both[count:] + dot(act_hi, outlo_ref[...])
    pred_grad = (predicted - noise_ref[...]) * weight_ref[...]
    pg_hi, pg_lo = two_parts(pred_grad)
    both = dot(jnp.concatenate([pg_hi, pg_lo], axis=0), outhi_t_ref[...])
    act_grad = both[:count] + both[count:] + dot(pg_hi, outlo_t_ref[...])
    scaled_grad = act_grad * gate * (1.0 + scaled * (1.0 - gate))
    gain_grad = jnp.sum(scaled_grad * unit, axis=0, keepdims=True)
    unit_grad = scaled_grad * gain
    along = jnp.mean(unit_grad * unit, axis=1, keepdims=True)
    hidden_grad = inverse * (unit_grad - unit * along)
    hg_hi, hg_lo = two_parts(hidden_grad)
    feats = feat_ref[...]
    half = feats.shape[0] // 2
    both = dot(feats, hg_hi)
    feat_grad = both[:half] + both[half:] + dot(feats[:half], hg_lo)
    turned = jnp.transpose(pred_grad)[:LAT]
    tg_hi, tg_lo = two_parts(turned)
    both = dot(jnp.concatenate([tg_hi, tg_lo], axis=0), act_hi)
    out_grad = both[:LAT] + both[LAT:] + dot(tg_hi, act_lo)
    cond_grad = hidden_grad[:rows]
    for draw in range(1, count // rows):
        cond_grad = cond_grad + hidden_grad[draw * rows : (draw + 1) * rows]
    block_scr[:, :width] = cond_grad
    block_scr[:, width:] = jnp.zeros((rows, EXTRA), F32)
    pieces = width // EXTRA
    for target in range(heads):
        source_rows = feat_grad if 2 * target < LAT else out_grad
        begin = 2 * target % LAT
        block_scr[rows - 2 : rows, :width] = source_rows[begin : begin + 2]
        if target < pieces:
            cols = slice(target * EXTRA, (target + 1) * EXTRA)
            block_scr[0:1, width:] = feat_grad[LAT : LAT + 1, cols]
            block_scr[1:2, width:] = gain_grad[:, cols]
        elif target == pieces:
            block_scr[:, width:] = jnp.zeros((rows, EXTRA), F32)
        send_ref[target] = block_scr[...].astype(BF16)


def grad_kernel(got_ref, picked_ref, after_ref, send_ref, pack_scr):
    heads, rows, wide = got_ref.shape
    width = wide - EXTRA
    groups = send_ref.shape[0]
    cond_grad = got_ref[:, :, :width].reshape(heads * rows, width)
    part = lax.dot_general(
        picked_ref[...], cond_grad, (((0,), (0,)), ((), ())), preferred_element_type=F32
    ).astype(BF16)
    summed = got_ref[0].astype(F32)
    for source in range(1, heads):
        summed = summed + got_ref[source].astype(F32)
    pack_scr[...] = jnp.zeros(pack_scr.shape, F32)
    pieces = width // 128
    for piece in range(pieces):
        row, lane = 2 * (piece % 8), 128 * (piece // 8)
        pack_scr[row : row + 2, lane : lane + 128] = summed[
            rows - 2 : rows, piece * 128 : (piece + 1) * 128
        ]
    row, lane = 2 * (pieces % 8), 128 * (pieces // 8)
    pack_scr[row : row + 2, lane : lane + 128] = summed[0:2, width:]
    packed = pack_scr[...].astype(BF16)
    row_groups = HD // GROUP_ROWS
    col_groups = groups // row_groups
    cols = width // col_groups
    for group in range(groups):
        top = group // col_groups * GROUP_ROWS
        left = group % col_groups * cols
        send_ref[group, :, :cols] = part[top : top + GROUP_ROWS, left : left + cols]
        send_ref[group, :, cols:] = packed


def total_kernel(got_ref, big_ref, small_ref):
    groups, rows, wide = got_ref.shape
    cols = wide - PACK
    total = got_ref[0].astype(F32)
    for source in range(1, groups):
        total = total + got_ref[source].astype(F32)
    rounded = total.astype(BF16)
    for group in range(groups):
        big_ref[group] = rounded[:, :cols]
    for head in range(small_ref.shape[0]):
        small_ref[head] = rounded[:, cols:]


def spread_kernel(big_ref, small_ref, cond_ref, in_ref, time_ref, gain_ref, out_ref):
    groups, rows, cols = big_ref.shape
    heads = small_ref.shape[0]
    width = cond_ref.shape[1]
    col_groups = width // cols
    for group in range(groups):
        top = group // col_groups * GROUP_ROWS
        left = group % col_groups * cols
        cond_ref[top : top + GROUP_ROWS, left : left + cols] = big_ref[group].astype(F32)
    pieces = width // 128
    for head in range(heads):
        packed = small_ref[head].astype(F32)
        target = in_ref if 2 * head < LAT else out_ref
        begin = 2 * head % LAT
        for piece in range(pieces):
            row, lane = 2 * (piece % 8), 128 * (piece // 8)
            target[begin : begin + 2, piece * 128 : (piece + 1) * 128] = packed[
                row : row + 2, lane : lane + 128
            ]
        if head < pieces:
            row, lane = 2 * (pieces % 8), 128 * (pieces // 8)
            cut = slice(head * 128, (head + 1) * 128)
            time_ref[:, cut] = packed[row : row + 1, lane : lane + 128]
            gain_ref[:, cut] = packed[row + 1 : row + 2, lane : lane + 128]


def call(kernel, out_shape, scratch, name, *operands, unread=0):
    specs = [vmem()] * (len(operands) - unread) + [anywhere()] * unread
    many = isinstance(out_shape, list)
    return pl.pallas_call(
        kernel,
        in_specs=specs,
        out_specs=[vmem()] * len(out_shape) if many else vmem(),
        out_shape=out_shape,
        scratch_shapes=scratch,
        compiler_params=params(),
        name=name,
    )(*operands)


def exchange(value, axis):
    return lax.all_to_all(value, axis, split_axis=0, concat_axis=0, tiled=True)


def local(
    queries, key_rows, value_rows, token_rank, masked_index, masked_counts, clean_latents,
    noise_draws, noise_times, w_cond, w_in, time_vec, norm_gain, w_out,
):
    each = queries.shape[0]
    heads = lax.axis_size("head")
    groups = lax.axis_size("seq")
    total = each * heads
    width = w_cond.shape[1]
    share = masked_index.shape[1] // heads
    count = DRAWS * SLOT

    stacked = jnp.stack([queries, key_rows, value_rows])
    stacked = jnp.transpose(stacked.reshape(3, each, heads, HD), (2, 0, 1, 3))
    arrived = exchange(stacked, "head")

    chosen = masked_index[0]
    live = lax.dynamic_index_in_dim(masked_counts, lax.axis_index("seq"), 0, keepdims=False)
    alive = jnp.arange(heads * share, dtype=jnp.int32) < live
    ranks = token_rank[0]

    def in_slots(value, fill):
        value = value.reshape(heads, share)
        return jnp.pad(value, ((0, 0), (0, SLOT - share)), constant_values=fill)

    where = in_slots(jnp.where(alive, chosen, -1), -1).reshape(heads * SLOT, 1)
    where_rank = in_slots(jnp.where(alive, jnp.take(ranks, chosen), -1), -1)
    where_rank = where_rank.reshape(heads * SLOT, 1)
    rank_row = ranks.reshape(1, total)
    rank_column = ranks.reshape(heads, each, 1)

    mine = lax.dynamic_index_in_dim(
        in_slots(chosen, 0), lax.axis_index("head"), 0, keepdims=False
    )
    my_alive = lax.dynamic_index_in_dim(
        in_slots(alive.astype(F32), 0.0), lax.axis_index("head"), 0, keepdims=False
    )
    clean = jnp.take(clean_latents, mine, axis=0).astype(F32)
    noise = jnp.take(noise_draws, mine, axis=0).astype(F32)
    times = jnp.take(noise_times, mine, axis=0).astype(F32)
    noise = jnp.transpose(noise.reshape(SLOT, DRAWS, LAT), (1, 0, 2))
    times = jnp.transpose(times)[:, :, None]
    angles = 0.5 * math.pi * times
    noisy = (jnp.cos(angles) * clean[None] + jnp.sin(angles) * noise).reshape(count, LAT)
    times = times.reshape(count, 1)
    noise = noise.reshape(count, LAT)
    base = jnp.dot(noisy, w_in, precision=lax.Precision.HIGHEST) + times * time_vec
    loss_scale = 1.0 / math.sqrt(masked_index.shape[1] // 3 * groups * DRAWS)
    row_weight = jnp.tile(my_alive * (2.0 * loss_scale), DRAWS).reshape(count, 1)
    feats = jnp.pad(jnp.concatenate([noisy, times], axis=1), ((0, 0), (0, 15))).T
    feats = jnp.concatenate(two_parts(feats), axis=0)
    out_wide = jnp.pad(w_out, ((0, 0), (0, 128 - LAT)))
    out_hi, out_lo = two_parts(out_wide)
    noise = jnp.pad(noise, ((0, 0), (0, 128 - LAT)))

    part, picked = attend_masked(arrived, where, where_rank, rank_row, w_cond)
    half = heads // 2
    got_cond = exchange(part, "head")
    first_half = attend_some(arrived, rank_column, rank_row, 0, half, part)

    send = call(
        head_kernel,
        jax.ShapeDtypeStruct((heads, SLOT, width + EXTRA), BF16),
        [pltpu.VMEM((SLOT, width + EXTRA), F32)],
        "diffusion_head",
        got_cond, base, norm_gain.reshape(1, width), out_hi, out_lo, out_hi.T, out_lo.T,
        noise, row_weight, feats, first_half,
        unread=1,
    )
    got_grad = exchange(send, "head")
    attended = attend_some(arrived, rank_column, rank_row, half, half, send, first_half)

    col_groups = groups // (HD // GROUP_ROWS)
    cols = width // col_groups
    parts = call(
        grad_kernel,
        jax.ShapeDtypeStruct((groups, GROUP_ROWS, cols + PACK), BF16),
        [pltpu.VMEM((GROUP_ROWS, PACK), F32)],
        "cond_weight_grad",
        got_grad, picked, attended,
        unread=1,
    )
    got_parts = exchange(parts, "seq")
    returned = exchange(attended, "head")
    big, small = call(
        total_kernel,
        [
            jax.ShapeDtypeStruct((groups, GROUP_ROWS, cols), BF16),
            jax.ShapeDtypeStruct((heads, GROUP_ROWS, PACK), BF16),
        ],
        [],
        "sum_over_clips",
        got_parts,
    )
    all_big = exchange(big, "seq")
    all_small = exchange(small, "head")
    cond_whole, in_grad, time_grad, gain_grad, out_grad = call(
        spread_kernel,
        [
            jax.ShapeDtypeStruct((HD, width), F32),
            jax.ShapeDtypeStruct((LAT, width), F32),
            jax.ShapeDtypeStruct((1, width), F32),
            jax.ShapeDtypeStruct((1, width), F32),
            jax.ShapeDtypeStruct((LAT, width), F32),
        ],
        [],
        "write_gradients",
        all_big, all_small,
    )
    attended_rows = jnp.transpose(returned, (1, 0, 2)).reshape(each, heads * HD)
    return (
        attended_rows, cond_whole, in_grad, time_grad.reshape(width),
        gain_grad.reshape(width), out_grad.T,
    )


def solution(mesh):
    return jax.shard_map(
        local,
        mesh=mesh,
        in_specs=(
            P(("seq", "head"), None),
            P(("seq", "head"), None),
            P(("seq", "head"), None),
            P("seq", None),
            P("seq", None),
            P(),
            P("seq", None),
            P("seq", None),
            P("seq", None),
            P("head", None),
            P(),
            P(),
            P(),
            P(),
        ),
        out_specs=(P(("seq", "head"), None), P("head", None), P(), P(), P(), P()),
        check_vma=False,
    )
```

```python
import functools
import math

import jax
import jax.numpy as jnp
from jax import lax
from jax.experimental import pallas as pl
from jax.experimental.pallas import tpu as pltpu
from jax.sharding import PartitionSpec as P

HD = 128
LAT = 16
DRAWS = 4
NORM_EPS = 1e-06
HIDDEN_SCORE = -1e30
SLOT = 16
EXTRA = 128
PACK = 256
TAIL = 32
GROUP_ROWS = 16
CHIPS_Y = 8
LOG2E = 1.4426950408889634
F32 = jnp.float32
BF16 = jnp.bfloat16
VMEM_LIMIT = 32 * 1024 * 1024


def params():
    return pltpu.CompilerParams(vmem_limit_bytes=VMEM_LIMIT)


def vmem():
    return pl.BlockSpec(memory_space=pltpu.VMEM)


def anywhere():
    return pl.BlockSpec(memory_space=pl.ANY)


def dot(a, b):
    return jnp.dot(a, b, preferred_element_type=F32)


def two_parts(value):
    high = value.astype(BF16)
    return high, (value - high.astype(F32)).astype(BF16)


def in_vmem(value):
    return pltpu.with_memory_space_constraint(value, pltpu.VMEM)


def stack_kernel(q_ref, k_ref, v_ref, out_ref):
    for head in range(out_ref.shape[0]):
        cols = slice(head * HD, (head + 1) * HD)
        out_ref[head, 0] = q_ref[:, cols]
        out_ref[head, 1] = k_ref[:, cols]
        out_ref[head, 2] = v_ref[:, cols]


def stack_by_head(queries, key_rows, value_rows, heads):
    each = queries.shape[0]
    block = heads // 4
    spec = pl.BlockSpec((each, block * HD), lambda i: (0, i))
    return pl.pallas_call(
        stack_kernel,
        grid=(4,),
        in_specs=[spec, spec, spec],
        out_specs=pl.BlockSpec((block, 3, each, HD), lambda i: (i, 0, 0, 0)),
        out_shape=jax.ShapeDtypeStruct((heads, 3, each, HD), BF16),
        compiler_params=params(),
        name="stack_by_head",
    )(queries, key_rows, value_rows)


def load_keys(got_ref, key_scr, val_scr):
    rows = key_scr.shape[0]
    key_scr[...] = got_ref[:, 1].reshape(rows, HD)
    val_scr[:, :HD] = got_ref[:, 2].reshape(rows, HD)
    val_scr[:, HD:] = jnp.ones((rows, HD), BF16)


def attend(query, query_rank, rank_ref, key_scr, val_scr, score_scr):
    total = key_scr.shape[0]
    chunk = math.gcd(total, 512)
    scale = LOG2E / math.sqrt(HD)
    top = None
    for start in range(0, total, chunk):
        scores = lax.dot_general(
            query,
            key_scr[start : start + chunk, :],
            (((1,), (1,)), ((), ())),
            preferred_element_type=F32,
        )
        visible = rank_ref[:, start : start + chunk] <= query_rank
        scores = jnp.where(visible, scores, HIDDEN_SCORE)
        score_scr[:, start : start + chunk] = scores
        for lane in range(0, chunk, 128):
            part = scores[:, lane : lane + 128]
            top = part if top is None else jnp.maximum(top, part)
    top = jnp.max(top, axis=1, keepdims=True)
    total_out = None
    for start in range(0, total, chunk):
        weights = jnp.exp2((score_scr[:, start : start + chunk] - top) * scale)
        mixed = dot(weights.astype(BF16), val_scr[start : start + chunk, :])
        total_out = mixed if total_out is None else total_out + mixed
    return total_out[:, :HD] / total_out[:, HD:]


def masked_kernel(got_ref, where_ref, qrank_ref, rank_ref, w_ref, *rest):
    part_ref, picked_ref, key_scr, val_scr, score_scr = rest[-5:]
    load_keys(got_ref, key_scr, val_scr)
    slots = where_ref.shape[0]
    total = key_scr.shape[0]
    sources, _, each, _ = got_ref.shape
    query = jnp.zeros((slots, HD), F32)
    step = math.gcd(each * sources, each * 4)
    for start in range(0, total, step):
        lanes = lax.broadcasted_iota(jnp.int32, (slots, step), 1) + start
        hit = jnp.where(lanes == where_ref[...], 1.0, 0.0).astype(BF16)
        rows = got_ref[start // each : (start + step) // each, 0].reshape(step, HD)
        query = query + dot(hit, rows)
    out = attend(query.astype(BF16), qrank_ref[...], rank_ref, key_scr, val_scr, score_scr)
    picked = jnp.where(qrank_ref[...] >= 0, out, 0.0).astype(BF16)
    picked_ref[...] = picked
    part = dot(picked, w_ref[...]).astype(BF16)
    part_ref[...] = part.reshape(part_ref.shape)


def attend_masked(arrived, where, where_rank, rank_row, w_cond, after):
    heads, _, each, _ = arrived.shape
    total = heads * each
    slots = where.shape[0]
    width = w_cond.shape[1]
    return pl.pallas_call(
        masked_kernel,
        in_specs=[vmem()] * 5 + [anywhere()] * len(after),
        out_specs=[vmem(), vmem()],
        out_shape=[
            jax.ShapeDtypeStruct((heads, slots // heads, width), BF16),
            jax.ShapeDtypeStruct((slots, HD), BF16),
        ],
        scratch_shapes=[
            pltpu.VMEM((total, HD), BF16),
            pltpu.VMEM((total, 2 * HD), BF16),
            pltpu.VMEM((slots, total), F32),
        ],
        compiler_params=params(),
        name="masked_rows",
    )(arrived, where, where_rank, rank_row, w_cond, *after)


def attend_kernel(first, got_ref, qrank_ref, rank_ref, *rest):
    out_ref, key_scr, val_scr, score_scr = rest[-4:]

    @pl.when(pl.program_id(0) == 0)
    def _():
        load_keys(got_ref, key_scr, val_scr)

    query = got_ref[pl.program_id(0) + first, 0]
    out = attend(query, qrank_ref[0], rank_ref, key_scr, val_scr, score_scr)
    out_ref[0] = out.astype(BF16)


def attend_some(arrived, rank_column, rank_row, first, count, after, earlier=None):
    heads, _, each, _ = arrived.shape
    total = heads * each
    specs = [
        vmem(),
        pl.BlockSpec((1, each, 1), lambda i: (i + first, 0, 0)),
        vmem(),
        anywhere(),
    ]
    operands = [arrived, rank_column, rank_row, after]
    aliases = {}
    if earlier is not None:
        specs.append(anywhere())
        operands.append(earlier)
        aliases = {len(operands) - 1: 0}
    return pl.pallas_call(
        functools.partial(attend_kernel, first),
        grid=(count,),
        in_specs=specs,
        out_specs=pl.BlockSpec((1, each, HD), lambda i: (i + first, 0, 0)),
        out_shape=jax.ShapeDtypeStruct((heads, each + TAIL, HD), BF16),
        scratch_shapes=[
            pltpu.VMEM((total, HD), BF16),
            pltpu.VMEM((total, 2 * HD), BF16),
            pltpu.VMEM((each, total), F32),
        ],
        input_output_aliases=aliases,
        compiler_params=params(),
        name="attention",
    )(*operands)


def head_kernel(
    cond_ref, base_ref, gain_ref, outhi_ref, outlo_ref, outhi_t_ref, outlo_t_ref, noise_ref,
    weight_ref, feat_ref, after_ref, send_ref, block_scr,
):
    heads, rows, width = cond_ref.shape
    count = base_ref.shape[0]
    condition = cond_ref[0].astype(F32)
    for source in range(1, heads):
        condition = condition + cond_ref[source].astype(F32)
    hidden = base_ref[...] + jnp.concatenate([condition] * (count // rows), axis=0)
    inverse = lax.rsqrt(jnp.mean(hidden * hidden, axis=1, keepdims=True) + NORM_EPS)
    unit = hidden * inverse
    gain = gain_ref[...]
    scaled = unit * gain
    gate = 1.0 / (1.0 + jnp.exp(-scaled))
    active = scaled * gate
    act_hi, act_lo = two_parts(active)
    both = dot(jnp.concatenate([act_hi, act_lo], axis=0), outhi_ref[...])
    predicted = both[:count] + both[count:] + dot(act_hi, outlo_ref[...])
    pred_grad = (predicted - noise_ref[...]) * weight_ref[...]
    pg_hi, pg_lo = two_parts(pred_grad)
    both = dot(jnp.concatenate([pg_hi, pg_lo], axis=0), outhi_t_ref[...])
    act_grad = both[:count] + both[count:] + dot(pg_hi, outlo_t_ref[...])
    scaled_grad = act_grad * gate * (1.0 + scaled * (1.0 - gate))
    gain_grad = jnp.sum(scaled_grad * unit, axis=0, keepdims=True)
    unit_grad = scaled_grad * gain
    along = jnp.mean(unit_grad * unit, axis=1, keepdims=True)
    hidden_grad = inverse * (unit_grad - unit * along)
    hg_hi, hg_lo = two_parts(hidden_grad)
    feats = feat_ref[...]
    half = feats.shape[0] // 2
    both = dot(feats, hg_hi)
    feat_grad = both[:half] + both[half:] + dot(feats[:half], hg_lo)
    turned = jnp.transpose(pred_grad)[:LAT]
    tg_hi, tg_lo = two_parts(turned)
    both = dot(jnp.concatenate([tg_hi, tg_lo], axis=0), act_hi)
    out_grad = both[:LAT] + both[LAT:] + dot(tg_hi, act_lo)
    cond_grad = hidden_grad[:rows]
    for draw in range(1, count // rows):
        cond_grad = cond_grad + hidden_grad[draw * rows : (draw + 1) * rows]
    block_scr[:, :width] = cond_grad
    block_scr[:, width:] = jnp.zeros((rows, EXTRA), F32)
    pieces = width // EXTRA
    for target in range(heads):
        source_rows = feat_grad if 2 * target < LAT else out_grad
        begin = 2 * target % LAT
        block_scr[rows - 2 : rows, :width] = source_rows[begin : begin + 2]
        if target < pieces:
            cols = slice(target * EXTRA, (target + 1) * EXTRA)
            block_scr[0:1, width:] = feat_grad[LAT : LAT + 1, cols]
            block_scr[1:2, width:] = gain_grad[:, cols]
        elif target == pieces:
            block_scr[:, width:] = jnp.zeros((rows, EXTRA), F32)
        send_ref[target] = block_scr[...].astype(BF16)


def grad_kernel(got_ref, picked_ref, after_ref, send_ref, pack_scr):
    heads, rows, wide = got_ref.shape
    width = wide - EXTRA
    groups = send_ref.shape[0]
    cond_grad = got_ref[:, :, :width].reshape(heads * rows, width)
    part = lax.dot_general(
        picked_ref[...], cond_grad, (((0,), (0,)), ((), ())), preferred_element_type=F32
    ).astype(BF16)
    summed = got_ref[0].astype(F32)
    for source in range(1, heads):
        summed = summed + got_ref[source].astype(F32)
    pack_scr[...] = jnp.zeros(pack_scr.shape, F32)
    pieces = width // 128
    for piece in range(pieces):
        row, lane = 2 * (piece % 8), 128 * (piece // 8)
        pack_scr[row : row + 2, lane : lane + 128] = summed[
            rows - 2 : rows, piece * 128 : (piece + 1) * 128
        ]
    row, lane = 2 * (pieces % 8), 128 * (pieces // 8)
    pack_scr[row : row + 2, lane : lane + 128] = summed[0:2, width:]
    packed = pack_scr[...].astype(BF16)
    row_groups = HD // GROUP_ROWS
    col_groups = groups // row_groups
    cols = width // col_groups
    for group in range(groups):
        top = group // col_groups * GROUP_ROWS
        left = group % col_groups * cols
        send_ref[group, :, :cols] = part[top : top + GROUP_ROWS, left : left + cols]
        send_ref[group, :, cols:] = packed


def total_kernel(got_ref, attended_ref, big_ref, tail_ref):
    groups, rows, wide = got_ref.shape
    cols = wide - PACK
    total = got_ref[0].astype(F32)
    for source in range(1, groups):
        total = total + got_ref[source].astype(F32)
    rounded = total.astype(BF16)
    big_ref[...] = rounded[:, :cols]
    for head in range(tail_ref.shape[0]):
        tail_ref[head, :rows] = rounded[:, cols : cols + HD]
        tail_ref[head, rows:] = rounded[:, cols + HD :]


def total_over_clips(got, attended, each):
    groups, rows, wide = got.shape
    heads = attended.shape[0]
    return pl.pallas_call(
        total_kernel,
        grid=(1,),
        in_specs=[vmem(), anywhere()],
        out_specs=[vmem(), pl.BlockSpec((heads, TAIL, HD), lambda i: (0, each // TAIL, 0))],
        out_shape=[
            jax.ShapeDtypeStruct((rows, wide - PACK), BF16),
            jax.ShapeDtypeStruct(attended.shape, BF16),
        ],
        input_output_aliases={1: 1},
        compiler_params=params(),
        name="sum_over_clips",
    )(got, attended)


def spread_kernel(seq_ref, *refs):
    big_refs = refs[:-6]
    tail_ref, cond_ref, in_ref, time_ref, gain_ref, out_ref = refs[-6:]
    far, rows, cols = big_refs[0].shape
    near = len(big_refs)
    heads = tail_ref.shape[0]
    width = cond_ref.shape[1]
    col_groups = width // cols
    seq = seq_ref[0]
    for back_y in range(near):
        for back_x in range(far):
            place_x = lax.rem(seq // near - back_x + far, far)
            place_y = lax.rem(lax.rem(seq, near) - back_y + near, near)
            group = place_x * near + place_y
            top = pl.multiple_of(group // col_groups * GROUP_ROWS, GROUP_ROWS)
            left = pl.multiple_of(lax.rem(group, col_groups) * cols, 128)
            piece = big_refs[back_y][back_x].astype(F32)
            cond_ref[pl.ds(top, GROUP_ROWS), pl.ds(left, cols)] = piece
    pieces = width // 128
    for head in range(heads):
        packed = tail_ref[head].astype(F32)
        target = in_ref if 2 * head < LAT else out_ref
        begin = 2 * head % LAT
        for piece in range(pieces):
            row = 2 * (piece % 8) + GROUP_ROWS * (piece // 8)
            target[begin : begin + 2, piece * 128 : (piece + 1) * 128] = packed[row : row + 2]
        if head < pieces:
            row = 2 * (pieces % 8) + GROUP_ROWS * (pieces // 8)
            cut = slice(head * 128, (head + 1) * 128)
            time_ref[cut] = packed[row]
            gain_ref[cut] = packed[row + 1]


def write_gradients(seq, big, returned, each, width):
    heads = returned.shape[0]
    return pl.pallas_call(
        spread_kernel,
        grid=(1,),
        in_specs=[
            pl.BlockSpec(memory_space=pltpu.SMEM),
            *[vmem()] * len(big),
            pl.BlockSpec((heads, TAIL, HD), lambda i: (0, each // TAIL, 0)),
        ],
        out_specs=[vmem()] * 5,
        out_shape=[
            jax.ShapeDtypeStruct((HD, width), F32),
            jax.ShapeDtypeStruct((LAT, width), F32),
            jax.ShapeDtypeStruct((width,), F32),
            jax.ShapeDtypeStruct((width,), F32),
            jax.ShapeDtypeStruct((LAT, width), F32),
        ],
        compiler_params=params(),
        name="write_gradients",
    )(seq, *big, returned)


def call(kernel, out_shape, scratch, name, *operands, unread=0):
    specs = [vmem()] * (len(operands) - unread) + [anywhere()] * unread
    many = isinstance(out_shape, list)
    return pl.pallas_call(
        kernel,
        in_specs=specs,
        out_specs=[vmem()] * len(out_shape) if many else vmem(),
        out_shape=out_shape,
        scratch_shapes=scratch,
        compiler_params=params(),
        name=name,
    )(*operands)


def shifted(value, groups, stride, radix, step):
    pairs = []
    for source in range(groups):
        digit = source // stride % radix
        pairs.append((source, source + ((digit + step) % radix - digit) * stride))
    return lax.ppermute(value, "seq", pairs)


def gather_over_clips(piece, groups):
    far = groups // CHIPS_Y
    over_x = [piece] + [shifted(piece, groups, CHIPS_Y, far, k) for k in range(1, far)]
    column = jnp.stack(over_x)
    return [column] + [shifted(column, groups, 1, CHIPS_Y, k) for k in range(1, CHIPS_Y)]


def exchange(value, axis):
    return lax.all_to_all(value, axis, split_axis=0, concat_axis=0, tiled=True)


def local(
    queries, key_rows, value_rows, token_rank, masked_index, masked_counts, clean_latents,
    noise_draws, noise_times, w_cond, w_in, time_vec, norm_gain, w_out,
):
    each = queries.shape[0]
    heads = lax.axis_size("head")
    groups = lax.axis_size("seq")
    total = each * heads
    width = w_cond.shape[1]
    share = masked_index.shape[1] // heads
    count = DRAWS * SLOT

    stacked = stack_by_head(queries, key_rows, value_rows, heads)
    arrived = in_vmem(exchange(stacked, "head"))

    chosen = masked_index[0]
    live = lax.dynamic_index_in_dim(masked_counts, lax.axis_index("seq"), 0, keepdims=False)
    alive = jnp.arange(heads * share, dtype=jnp.int32) < live
    ranks = token_rank[0]

    def in_slots(value, fill):
        value = value.reshape(heads, share)
        return jnp.pad(value, ((0, 0), (0, SLOT - share)), constant_values=fill)

    where = in_slots(jnp.where(alive, chosen, -1), -1).reshape(heads * SLOT, 1)
    where_rank = in_slots(jnp.where(alive, jnp.take(ranks, chosen), -1), -1)
    where_rank = where_rank.reshape(heads * SLOT, 1)
    rank_row = ranks.reshape(1, total)
    rank_column = ranks.reshape(heads, each, 1)

    mine = lax.dynamic_index_in_dim(
        in_slots(chosen, 0), lax.axis_index("head"), 0, keepdims=False
    )
    my_alive = lax.dynamic_index_in_dim(
        in_slots(alive.astype(F32), 0.0), lax.axis_index("head"), 0, keepdims=False
    )
    clean = jnp.take(clean_latents, mine, axis=0).astype(F32)
    noise = jnp.take(noise_draws, mine, axis=0).astype(F32)
    times = jnp.take(noise_times, mine, axis=0).astype(F32)
    noise = jnp.transpose(noise.reshape(SLOT, DRAWS, LAT), (1, 0, 2))
    times = jnp.transpose(times)[:, :, None]
    angles = 0.5 * math.pi * times
    noisy = (jnp.cos(angles) * clean[None] + jnp.sin(angles) * noise).reshape(count, LAT)
    times = times.reshape(count, 1)
    noise = noise.reshape(count, LAT)
    base = jnp.dot(noisy, w_in, precision=lax.Precision.HIGHEST) + times * time_vec
    loss_scale = 1.0 / math.sqrt(masked_index.shape[1] // 3 * groups * DRAWS)
    row_weight = jnp.tile(my_alive * (2.0 * loss_scale), DRAWS).reshape(count, 1)
    feats = jnp.pad(jnp.concatenate([noisy, times], axis=1), ((0, 0), (0, 15))).T
    feats = jnp.concatenate(two_parts(feats), axis=0)
    out_wide = jnp.pad(w_out, ((0, 0), (0, 128 - LAT)))
    out_hi, out_lo = two_parts(out_wide)
    noise = jnp.pad(noise, ((0, 0), (0, 128 - LAT)))

    prepared = (
        base, norm_gain.reshape(1, width), out_hi, out_lo, out_hi.T, out_lo.T, noise,
        row_weight, feats,
    )
    part, picked = attend_masked(
        arrived, where, where_rank, rank_row, w_cond, (*prepared, rank_column)
    )
    half = heads // 2
    got_cond = exchange(part, "head")
    first_half = attend_some(arrived, rank_column, rank_row, 0, half, part)

    send = call(
        head_kernel,
        jax.ShapeDtypeStruct((heads, SLOT, width + EXTRA), BF16),
        [pltpu.VMEM((SLOT, width + EXTRA), F32)],
        "diffusion_head",
        in_vmem(got_cond), *prepared, first_half,
        unread=1,
    )
    got_grad = exchange(send, "head")
    attended = attend_some(arrived, rank_column, rank_row, half, half, send, first_half)

    col_groups = groups // (HD // GROUP_ROWS)
    cols = width // col_groups
    parts = call(
        grad_kernel,
        jax.ShapeDtypeStruct((groups, GROUP_ROWS, cols + PACK), BF16),
        [pltpu.VMEM((GROUP_ROWS, PACK), F32)],
        "cond_weight_grad",
        in_vmem(got_grad), picked, attended,
        unread=1,
    )
    got_parts = exchange(parts, "seq")
    big, message = total_over_clips(in_vmem(got_parts), attended, each)
    returned = exchange(message, "head")
    all_big = gather_over_clips(big, groups)
    cond_whole, in_grad, time_grad, gain_grad, out_grad = write_gradients(
        lax.axis_index("seq").reshape(1), all_big, returned, each, width
    )
    rows = jnp.transpose(returned[:, :each], (1, 0, 2)).reshape(each, heads * HD)
    return (rows, cond_whole, in_grad, time_grad, gain_grad, out_grad.T)


def solution(mesh):
    return jax.shard_map(
        local,
        mesh=mesh,
        in_specs=(
            P(("seq", "head"), None),
            P(("seq", "head"), None),
            P(("seq", "head"), None),
            P("seq", None),
            P("seq", None),
            P(),
            P("seq", None),
            P("seq", None),
            P("seq", None),
            P("head", None),
            P(),
            P(),
            P(),
            P(),
        ),
        out_specs=(P(("seq", "head"), None), P("head", None), P(), P(), P(), P()),
        check_vma=False,
    )
```

```python
import functools
import math

import jax
import jax.numpy as jnp
from jax import lax
from jax.experimental import pallas as pl
from jax.experimental.pallas import tpu as pltpu
from jax.sharding import PartitionSpec as P

HD = 128
LAT = 16
DRAWS = 4
NORM_EPS = 1e-06
HIDDEN_SCORE = -1e30
SLOT = 16
EXTRA = 128
PACK = 256
TAIL = 32
GROUP_ROWS = 16
STRIDES = (4, 16, 2, 8, 1)
LOG2E = 1.4426950408889634
F32 = jnp.float32
BF16 = jnp.bfloat16
VMEM_LIMIT = 32 * 1024 * 1024


def params():
    return pltpu.CompilerParams(vmem_limit_bytes=VMEM_LIMIT)


def vmem():
    return pl.BlockSpec(memory_space=pltpu.VMEM)


def anywhere():
    return pl.BlockSpec(memory_space=pl.ANY)


def dot(a, b):
    return jnp.dot(a, b, preferred_element_type=F32)


def dot_rows(a, b):
    return lax.dot_general(a, b, (((1,), (1,)), ((), ())), preferred_element_type=F32)


def dot_over_rows(a, b):
    return lax.dot_general(a, b, (((0,), (0,)), ((), ())), preferred_element_type=F32)


def two_parts(value):
    high = value.astype(BF16)
    return high, (value - high.astype(F32)).astype(BF16)


def in_vmem(value):
    return pltpu.with_memory_space_constraint(value, pltpu.VMEM)


def in_hbm(value):
    return pltpu.with_memory_space_constraint(value, pltpu.HBM)


def stack_kernel(q_ref, k_ref, v_ref, out_ref):
    for head in range(out_ref.shape[0]):
        cols = slice(head * HD, (head + 1) * HD)
        out_ref[head, 0] = q_ref[:, cols]
        out_ref[head, 1] = k_ref[:, cols]
        out_ref[head, 2] = v_ref[:, cols]


def stack_by_head(queries, key_rows, value_rows, heads):
    each = queries.shape[0]
    block = heads // 4
    spec = pl.BlockSpec((each, block * HD), lambda i: (0, i))
    return pl.pallas_call(
        stack_kernel,
        grid=(4,),
        in_specs=[spec, spec, spec],
        out_specs=pl.BlockSpec((block, 3, each, HD), lambda i: (i, 0, 0, 0)),
        out_shape=pltpu.HBM((heads, 3, each, HD), BF16),
        compiler_params=params(),
        name="stack_by_head",
    )(in_hbm(queries), in_hbm(key_rows), in_hbm(value_rows))


def load_keys(got_ref, key_scr, val_scr):
    rows = key_scr.shape[0]
    key_scr[...] = got_ref[:, 1].reshape(rows, HD)
    val_scr[:, :HD] = got_ref[:, 2].reshape(rows, HD)
    val_scr[:, HD:] = jnp.ones((rows, HD), BF16)


def attend(query, query_rank, rank_ref, key_scr, val_scr, score_scr):
    total = key_scr.shape[0]
    chunk = math.gcd(total, 512)
    scale = LOG2E / math.sqrt(HD)
    top = None
    for start in range(0, total, chunk):
        scores = lax.dot_general(
            query,
            key_scr[start : start + chunk, :],
            (((1,), (1,)), ((), ())),
            preferred_element_type=F32,
        )
        visible = rank_ref[:, start : start + chunk] <= query_rank
        scores = jnp.where(visible, scores, HIDDEN_SCORE)
        score_scr[:, start : start + chunk] = scores
        for lane in range(0, chunk, 128):
            part = scores[:, lane : lane + 128]
            top = part if top is None else jnp.maximum(top, part)
    top = jnp.max(top, axis=1, keepdims=True)
    total_out = None
    for start in range(0, total, chunk):
        weights = jnp.exp2((score_scr[:, start : start + chunk] - top) * scale)
        mixed = dot(weights.astype(BF16), val_scr[start : start + chunk, :])
        total_out = mixed if total_out is None else total_out + mixed
    return total_out[:, :HD] / total_out[:, HD:]


def masked_kernel(got_ref, where_ref, qrank_ref, rank_ref, w_ref, *rest):
    part_ref, picked_ref, key_scr, val_scr, score_scr, w_scr, sem = rest
    fetch = pltpu.make_async_copy(w_ref, w_scr, sem)
    fetch.start()
    load_keys(got_ref, key_scr, val_scr)
    slots = where_ref.shape[0]
    total = key_scr.shape[0]
    sources, _, each, _ = got_ref.shape
    query = jnp.zeros((slots, HD), F32)
    step = math.gcd(each * sources, each * 4)
    for start in range(0, total, step):
        lanes = lax.broadcasted_iota(jnp.int32, (slots, step), 1) + start
        hit = jnp.where(lanes == where_ref[...], 1.0, 0.0).astype(BF16)
        rows = got_ref[start // each : (start + step) // each, 0].reshape(step, HD)
        query = query + dot(hit, rows)
    out = attend(query.astype(BF16), qrank_ref[...], rank_ref, key_scr, val_scr, score_scr)
    picked = jnp.where(qrank_ref[...] >= 0, out, 0.0).astype(BF16)
    picked_ref[...] = picked
    fetch.wait()
    part = dot(picked, w_scr[...]).astype(BF16)
    part_ref[...] = part.reshape(part_ref.shape)


def attend_masked(arrived, where, where_rank, rank_row, w_cond):
    heads, _, each, _ = arrived.shape
    total = heads * each
    slots = where.shape[0]
    width = w_cond.shape[1]
    return pl.pallas_call(
        masked_kernel,
        in_specs=[vmem()] * 4 + [anywhere()],
        out_specs=[vmem(), vmem()],
        out_shape=[
            pltpu.HBM((heads, slots // heads, width), BF16),
            jax.ShapeDtypeStruct((slots, HD), BF16),
        ],
        scratch_shapes=[
            pltpu.VMEM((total, HD), BF16),
            pltpu.VMEM((total, 2 * HD), BF16),
            pltpu.VMEM((slots, total), F32),
            pltpu.VMEM(w_cond.shape, BF16),
            pltpu.SemaphoreType.DMA,
        ],
        compiler_params=params(),
        name="masked_rows",
    )(arrived, where, where_rank, rank_row, in_hbm(w_cond))


def attend_kernel(first, got_ref, qrank_ref, rank_ref, *rest):
    out_ref, key_scr, val_scr, score_scr = rest[-4:]

    @pl.when(pl.program_id(0) == 0)
    def _():
        load_keys(got_ref, key_scr, val_scr)

    source = pl.program_id(0) + first
    columns = qrank_ref[...]
    lanes = lax.broadcasted_iota(jnp.int32, columns.shape, 1)
    ranks = jnp.sum(jnp.where(lanes == source, columns, 0), axis=1, keepdims=True)
    out = attend(got_ref[source, 0], ranks, rank_ref, key_scr, val_scr, score_scr)
    out_ref[0] = out.astype(BF16)


def attend_some(arrived, rank_columns, rank_row, first, count, after, earlier=None):
    heads, _, each, _ = arrived.shape
    total = heads * each
    specs = [
        vmem(),
        vmem(),
        vmem(),
        anywhere(),
    ]
    operands = [arrived, rank_columns, rank_row, after]
    aliases = {}
    if earlier is not None:
        specs.append(anywhere())
        operands.append(earlier)
        aliases = {len(operands) - 1: 0}
    return pl.pallas_call(
        functools.partial(attend_kernel, first),
        grid=(count,),
        in_specs=specs,
        out_specs=pl.BlockSpec((1, each, HD), lambda i: (i + first, 0, 0)),
        out_shape=jax.ShapeDtypeStruct((heads, each + TAIL, HD), BF16),
        scratch_shapes=[
            pltpu.VMEM((total, HD), BF16),
            pltpu.VMEM((total, 2 * HD), BF16),
            pltpu.VMEM((each, total), F32),
        ],
        input_output_aliases=aliases,
        compiler_params=params(),
        name="attention",
    )(*operands)


def head_kernel(
    cond_ref, base_ref, gain_ref, out_t_ref, noise_ref, weight_ref, feat_ref, after_ref,
    send_ref, token_ref, block_scr,
):
    heads, rows, width = cond_ref.shape
    count = base_ref.shape[0]
    condition = cond_ref[0].astype(F32)
    for source in range(1, heads):
        condition = condition + cond_ref[source].astype(F32)
    hidden = base_ref[...] + jnp.concatenate([condition] * (count // rows), axis=0)
    inverse = lax.rsqrt(jnp.mean(hidden * hidden, axis=1, keepdims=True) + NORM_EPS)
    unit = hidden * inverse
    gain = gain_ref[...]
    scaled = unit * gain
    gate = 1.0 / (1.0 + jnp.exp(-scaled))
    active = scaled * gate
    act_hi, act_lo = two_parts(active)
    out_hi, out_lo = two_parts(out_t_ref[...])
    both = dot_rows(jnp.concatenate([act_hi, act_lo], axis=0), out_hi)
    predicted = both[:count] + both[count:] + dot_rows(act_hi, out_lo)
    pred_grad = (predicted - noise_ref[...]) * weight_ref[...]
    pg_hi, pg_lo = two_parts(pred_grad)
    both = dot(jnp.concatenate([pg_hi, pg_lo], axis=0), out_hi)
    act_grad = both[:count] + both[count:] + dot(pg_hi, out_lo)
    scaled_grad = act_grad * gate * (1.0 + scaled * (1.0 - gate))
    gain_grad = jnp.sum(scaled_grad * unit, axis=0, keepdims=True)
    unit_grad = scaled_grad * gain
    along = jnp.mean(unit_grad * unit, axis=1, keepdims=True)
    hidden_grad = inverse * (unit_grad - unit * along)
    hg_hi, hg_lo = two_parts(hidden_grad)
    feats = feat_ref[...]
    half = feats.shape[0] // 2
    both = dot(feats, hg_hi)
    feat_grad = both[:half] + both[half:] + dot(feats[:half], hg_lo)
    out_grad = dot_over_rows(pg_hi, act_hi) + dot_over_rows(pg_lo, act_hi)
    out_grad = out_grad + dot_over_rows(pg_hi, act_lo)
    token_ref[...] = inverse[:8] + jnp.zeros(token_ref.shape, F32)
    cond_grad = hidden_grad[:rows]
    for draw in range(1, count // rows):
        cond_grad = cond_grad + hidden_grad[draw * rows : (draw + 1) * rows]
    block_scr[:, :width] = cond_grad
    block_scr[:, width:] = jnp.zeros((rows, EXTRA), F32)
    pieces = width // EXTRA
    for target in range(heads):
        source_rows = feat_grad if 2 * target < LAT else out_grad
        begin = 2 * target % LAT
        block_scr[rows - 2 : rows, :width] = source_rows[begin : begin + 2]
        if target < pieces:
            cols = slice(target * EXTRA, (target + 1) * EXTRA)
            block_scr[0:1, width:] = feat_grad[LAT : LAT + 1, cols]
            block_scr[1:2, width:] = gain_grad[:, cols]
        elif target == pieces:
            block_scr[:, width:] = jnp.zeros((rows, EXTRA), F32)
        send_ref[target] = block_scr[...].astype(BF16)


def grad_kernel(got_ref, picked_ref, after_ref, send_ref, pack_scr):
    heads, rows, wide = got_ref.shape
    width = wide - EXTRA
    groups = send_ref.shape[0]
    cond_grad = got_ref[:, :, :width].reshape(heads * rows, width)
    part = lax.dot_general(
        picked_ref[...], cond_grad, (((0,), (0,)), ((), ())), preferred_element_type=F32
    ).astype(BF16)
    summed = got_ref[0].astype(F32)
    for source in range(1, heads):
        summed = summed + got_ref[source].astype(F32)
    pack_scr[...] = jnp.zeros(pack_scr.shape, F32)
    pieces = width // 128
    for piece in range(pieces):
        row, lane = 2 * (piece % 8), 128 * (piece // 8)
        pack_scr[row : row + 2, lane : lane + 128] = summed[
            rows - 2 : rows, piece * 128 : (piece + 1) * 128
        ]
    row, lane = 2 * (pieces % 8), 128 * (pieces // 8)
    pack_scr[row : row + 2, lane : lane + 128] = summed[0:2, width:]
    packed = pack_scr[...].astype(BF16)
    row_groups = HD // GROUP_ROWS
    col_groups = groups // row_groups
    cols = width // col_groups
    for group in range(groups):
        top = group // col_groups * GROUP_ROWS
        left = group % col_groups * cols
        send_ref[group, :, :cols] = part[top : top + GROUP_ROWS, left : left + cols]
        send_ref[group, :, cols:] = packed


def total_kernel(got_ref, attended_ref, big_ref, tail_ref):
    groups, rows, wide = got_ref.shape
    cols = wide - PACK
    total = got_ref[0].astype(F32)
    for source in range(1, groups):
        total = total + got_ref[source].astype(F32)
    rounded = total.astype(BF16)
    big_ref[...] = rounded[:, :cols]
    for head in range(tail_ref.shape[0]):
        tail_ref[head, :rows] = rounded[:, cols : cols + HD]
        tail_ref[head, rows:] = rounded[:, cols + HD :]


def total_over_clips(got, attended, each):
    groups, rows, wide = got.shape
    heads = attended.shape[0]
    return pl.pallas_call(
        total_kernel,
        grid=(1,),
        in_specs=[vmem(), anywhere()],
        out_specs=[vmem(), pl.BlockSpec((heads, TAIL, HD), lambda i: (0, each // TAIL, 0))],
        out_shape=[
            jax.ShapeDtypeStruct((rows, wide - PACK), BF16),
            jax.ShapeDtypeStruct(attended.shape, BF16),
        ],
        input_output_aliases={1: 1},
        compiler_params=params(),
        name="sum_over_clips",
    )(got, attended)


def spread_kernel(
    strides, seq_ref, big_ref, tail_ref, cond_ref, in_ref, time_ref, gain_ref, out_ref
):
    groups, rows, cols = big_ref.shape
    heads = tail_ref.shape[0]
    width = cond_ref.shape[1]
    col_groups = width // cols
    seq = seq_ref[0]
    for place in range(groups):
        apart = sum(stride for bit, stride in enumerate(strides) if place >> bit & 1)
        group = seq ^ apart
        top = pl.multiple_of(group // col_groups * GROUP_ROWS, GROUP_ROWS)
        left = pl.multiple_of(lax.rem(group, col_groups) * cols, 128)
        cond_ref[pl.ds(top, GROUP_ROWS), pl.ds(left, cols)] = big_ref[place].astype(F32)
    pieces = width // 128
    for head in range(heads):
        packed = tail_ref[head].astype(F32)
        target = in_ref if 2 * head < LAT else out_ref
        begin = 2 * head % LAT
        for piece in range(pieces):
            row = 2 * (piece % 8) + GROUP_ROWS * (piece // 8)
            target[begin : begin + 2, piece * 128 : (piece + 1) * 128] = packed[row : row + 2]
        if head < pieces:
            row = 2 * (pieces % 8) + GROUP_ROWS * (pieces // 8)
            cut = slice(head * 128, (head + 1) * 128)
            time_ref[cut] = packed[row]
            gain_ref[cut] = packed[row + 1]


def write_gradients(seq, big, strides, returned, each, width):
    heads = returned.shape[0]
    return pl.pallas_call(
        functools.partial(spread_kernel, strides),
        grid=(1,),
        in_specs=[
            pl.BlockSpec(memory_space=pltpu.SMEM),
            vmem(),
            pl.BlockSpec((heads, TAIL, HD), lambda i: (0, each // TAIL, 0)),
        ],
        out_specs=[vmem()] * 5,
        out_shape=[
            jax.ShapeDtypeStruct((HD, width), F32),
            jax.ShapeDtypeStruct((LAT, width), F32),
            jax.ShapeDtypeStruct((width,), F32),
            jax.ShapeDtypeStruct((width,), F32),
            jax.ShapeDtypeStruct((LAT, width), F32),
        ],
        compiler_params=params(),
        name="write_gradients",
    )(seq, big, returned)


def call(kernel, out_shape, scratch, name, *operands, unread=0):
    specs = [vmem()] * (len(operands) - unread) + [anywhere()] * unread
    many = isinstance(out_shape, list)
    return pl.pallas_call(
        kernel,
        in_specs=specs,
        out_specs=[vmem()] * len(out_shape) if many else vmem(),
        out_shape=out_shape,
        scratch_shapes=scratch,
        compiler_params=params(),
        name=name,
    )(*operands)


def gather_over_clips(piece, groups):
    held = piece[None]
    strides = []
    for stride in STRIDES:
        if stride < groups:
            pairs = [(source, source ^ stride) for source in range(groups)]
            held = jnp.concatenate([held, lax.ppermute(held, "seq", pairs)])
            strides.append(stride)
    return held, strides


def exchange(value, axis):
    return lax.all_to_all(value, axis, split_axis=0, concat_axis=0, tiled=True)


def local(
    queries, key_rows, value_rows, token_rank, masked_index, masked_counts, clean_latents,
    noise_draws, noise_times, w_cond, w_in, time_vec, norm_gain, w_out,
):
    each = queries.shape[0]
    heads = lax.axis_size("head")
    groups = lax.axis_size("seq")
    total = each * heads
    width = w_cond.shape[1]
    share = masked_index.shape[1] // heads
    count = DRAWS * SLOT

    stacked = stack_by_head(queries, key_rows, value_rows, heads)
    arrived = in_vmem(exchange(stacked, "head"))

    chosen = masked_index[0]
    live = lax.dynamic_index_in_dim(masked_counts, lax.axis_index("seq"), 0, keepdims=False)
    alive = jnp.arange(heads * share, dtype=jnp.int32) < live
    ranks = token_rank[0]

    def in_slots(value, fill):
        value = value.reshape(heads, share)
        return jnp.pad(value, ((0, 0), (0, SLOT - share)), constant_values=fill)

    where = in_slots(jnp.where(alive, chosen, -1), -1).reshape(heads * SLOT, 1)
    where_rank = in_slots(jnp.where(alive, jnp.take(ranks, chosen), -1), -1)
    where_rank = where_rank.reshape(heads * SLOT, 1)
    rank_row = ranks.reshape(1, total)
    rank_columns = jnp.pad(ranks.reshape(heads, each).T, ((0, 0), (0, 128 - heads)))

    mine = lax.dynamic_index_in_dim(
        in_slots(chosen, 0), lax.axis_index("head"), 0, keepdims=False
    )
    my_alive = lax.dynamic_index_in_dim(
        in_slots(alive.astype(F32), 0.0), lax.axis_index("head"), 0, keepdims=False
    )
    clean = jnp.take(clean_latents, mine, axis=0).astype(F32)
    noise = jnp.take(noise_draws, mine, axis=0).astype(F32)
    times = jnp.take(noise_times, mine, axis=0).astype(F32)
    noise = jnp.transpose(noise.reshape(SLOT, DRAWS, LAT), (1, 0, 2))
    times = jnp.transpose(times)[:, :, None]
    angles = 0.5 * math.pi * times
    noisy = (jnp.cos(angles) * clean[None] + jnp.sin(angles) * noise).reshape(count, LAT)
    times = times.reshape(count, 1)
    noise = noise.reshape(count, LAT)
    base = jnp.dot(noisy, w_in, precision=lax.Precision.HIGHEST) + times * time_vec
    loss_scale = 1.0 / math.sqrt(masked_index.shape[1] // 3 * groups * DRAWS)
    row_weight = jnp.tile(my_alive * (2.0 * loss_scale), DRAWS).reshape(count, 1)
    feats = jnp.pad(jnp.concatenate([noisy, times], axis=1), ((0, 0), (0, 15))).T
    feats = jnp.concatenate(two_parts(feats), axis=0)

    where_rank, rank_columns, base, noise, row_weight, feats = lax.optimization_barrier(
        (where_rank, rank_columns, base, noise, row_weight, feats)
    )
    part, picked = attend_masked(arrived, where, where_rank, rank_row, w_cond)
    half = heads // 2
    got_cond = exchange(part, "head")
    first_half = attend_some(arrived, rank_columns, rank_row, 0, half, picked)

    send, token = call(
        head_kernel,
        [
            pltpu.HBM((heads, SLOT, width + EXTRA), BF16),
            jax.ShapeDtypeStruct((8, 128), F32),
        ],
        [pltpu.VMEM((SLOT, width + EXTRA), F32)],
        "diffusion_head",
        in_vmem(got_cond), base, norm_gain.reshape(1, width), w_out.T, noise, row_weight,
        feats, first_half,
        unread=1,
    )
    got_grad = exchange(send, "head")
    attended = attend_some(arrived, rank_columns, rank_row, half, half, token, first_half)

    col_groups = groups // (HD // GROUP_ROWS)
    cols = width // col_groups
    parts = call(
        grad_kernel,
        jax.ShapeDtypeStruct((groups, GROUP_ROWS, cols + PACK), BF16),
        [pltpu.VMEM((GROUP_ROWS, PACK), F32)],
        "cond_weight_grad",
        in_vmem(got_grad), picked, attended,
        unread=1,
    )
    got_parts = exchange(parts, "seq")
    big, message = total_over_clips(in_vmem(got_parts), attended, each)
    returned = exchange(message, "head")
    all_big, strides = gather_over_clips(big, groups)
    cond_whole, in_grad, time_grad, gain_grad, out_grad = write_gradients(
        lax.axis_index("seq").reshape(1), all_big, strides, returned, each, width
    )
    rows = jnp.transpose(returned[:, :each], (1, 0, 2)).reshape(each, heads * HD)
    return (rows, cond_whole, in_grad, time_grad, gain_grad, out_grad.T)


def solution(mesh):
    return jax.shard_map(
        local,
        mesh=mesh,
        in_specs=(
            P(("seq", "head"), None),
            P(("seq", "head"), None),
            P(("seq", "head"), None),
            P("seq", None),
            P("seq", None),
            P(),
            P("seq", None),
            P("seq", None),
            P("seq", None),
            P("head", None),
            P(),
            P(),
            P(),
            P(),
        ),
        out_specs=(P(("seq", "head"), None), P("head", None), P(), P(), P(), P()),
        check_vma=False,
    )
```

```python
import functools
import math

import jax
import jax.numpy as jnp
from jax import lax
from jax.experimental import pallas as pl
from jax.experimental.pallas import tpu as pltpu
from jax.sharding import PartitionSpec as P

HD = 128
LAT = 16
DRAWS = 4
NORM_EPS = 1e-06
HIDDEN_SCORE = -1e30
SLOT = 16
EXTRA = 128
PACK = 256
TAIL = 32
GROUP_ROWS = 16
LOG2E = 1.4426950408889634
F32 = jnp.float32
BF16 = jnp.bfloat16
VMEM_LIMIT = 32 * 1024 * 1024


def params():
    return pltpu.CompilerParams(vmem_limit_bytes=VMEM_LIMIT)


def vmem():
    return pl.BlockSpec(memory_space=pltpu.VMEM)


def anywhere():
    return pl.BlockSpec(memory_space=pl.ANY)


def dot(a, b):
    return jnp.dot(a, b, preferred_element_type=F32)


def dot_rows(a, b):
    return lax.dot_general(a, b, (((1,), (1,)), ((), ())), preferred_element_type=F32)


def dot_over_rows(a, b):
    return lax.dot_general(a, b, (((0,), (0,)), ((), ())), preferred_element_type=F32)


def two_parts(value):
    high = value.astype(BF16)
    return high, (value - high.astype(F32)).astype(BF16)


def in_vmem(value):
    return pltpu.with_memory_space_constraint(value, pltpu.VMEM)


def in_hbm(value):
    return pltpu.with_memory_space_constraint(value, pltpu.HBM)


def stack_kernel(q_ref, k_ref, v_ref, out_ref):
    for head in range(out_ref.shape[0]):
        cols = slice(head * HD, (head + 1) * HD)
        out_ref[head, 0] = q_ref[:, cols]
        out_ref[head, 1] = k_ref[:, cols]
        out_ref[head, 2] = v_ref[:, cols]


def stack_by_head(queries, key_rows, value_rows, heads):
    each = queries.shape[0]
    block = each // 2
    spec = pl.BlockSpec((block, heads * HD), lambda i: (i, 0))
    return pl.pallas_call(
        stack_kernel,
        grid=(2,),
        in_specs=[spec, spec, spec],
        out_specs=pl.BlockSpec((heads, 3, block, HD), lambda i: (0, 0, i, 0)),
        out_shape=pltpu.HBM((heads, 3, each, HD), BF16),
        compiler_params=params(),
        name="stack_by_head",
    )(in_hbm(queries), in_hbm(key_rows), in_hbm(value_rows))


def load_keys(got_ref, key_scr, val_scr):
    rows = key_scr.shape[0]
    key_scr[...] = got_ref[:, 1].reshape(rows, HD)
    val_scr[:, :HD] = got_ref[:, 2].reshape(rows, HD)
    val_scr[:, HD:] = jnp.ones((rows, HD), BF16)


def attend(query, query_rank, rank_ref, key_scr, val_scr, score_scr):
    total = key_scr.shape[0]
    chunk = math.gcd(total, 512)
    scale = LOG2E / math.sqrt(HD)
    top = None
    for start in range(0, total, chunk):
        scores = lax.dot_general(
            query,
            key_scr[start : start + chunk, :],
            (((1,), (1,)), ((), ())),
            preferred_element_type=F32,
        )
        visible = rank_ref[:, start : start + chunk] <= query_rank
        scores = jnp.where(visible, scores, HIDDEN_SCORE)
        score_scr[:, start : start + chunk] = scores
        for lane in range(0, chunk, 128):
            part = scores[:, lane : lane + 128]
            top = part if top is None else jnp.maximum(top, part)
    top = jnp.max(top, axis=1, keepdims=True)
    total_out = None
    for start in range(0, total, chunk):
        weights = jnp.exp2((score_scr[:, start : start + chunk] - top) * scale)
        mixed = dot(weights.astype(BF16), val_scr[start : start + chunk, :])
        total_out = mixed if total_out is None else total_out + mixed
    return total_out[:, :HD] / total_out[:, HD:]


def masked_kernel(got_ref, slot_ref, rank_ref, w_ref, *rest):
    part_ref, picked_ref, key_scr, val_scr, score_scr, w_scr, sem = rest
    fetch = pltpu.make_async_copy(w_ref, w_scr, sem)
    fetch.start()
    load_keys(got_ref, key_scr, val_scr)
    slots = slot_ref.shape[0]
    where = slot_ref[:, 0:1]
    slot_rank = slot_ref[:, 1:2]
    total = key_scr.shape[0]
    sources, _, each, _ = got_ref.shape
    query = jnp.zeros((slots, HD), F32)
    step = math.gcd(each * sources, each * 4)
    for start in range(0, total, step):
        lanes = lax.broadcasted_iota(jnp.int32, (slots, step), 1) + start
        hit = jnp.where(lanes == where, 1.0, 0.0).astype(BF16)
        rows = got_ref[start // each : (start + step) // each, 0].reshape(step, HD)
        query = query + dot(hit, rows)
    out = attend(query.astype(BF16), slot_rank, rank_ref, key_scr, val_scr, score_scr)
    picked = jnp.where(slot_rank >= 0, out, 0.0).astype(BF16)
    picked_ref[...] = picked
    fetch.wait()
    part = dot(picked, w_scr[...]).astype(BF16)
    part_ref[...] = part.reshape(part_ref.shape)


def attend_masked(arrived, slot_columns, rank_row, w_cond):
    heads, _, each, _ = arrived.shape
    total = heads * each
    slots = slot_columns.shape[0]
    width = w_cond.shape[1]
    return pl.pallas_call(
        masked_kernel,
        in_specs=[vmem()] * 3 + [anywhere()],
        out_specs=[vmem(), vmem()],
        out_shape=[
            pltpu.HBM((heads, slots // heads, width), BF16),
            jax.ShapeDtypeStruct((slots, HD), BF16),
        ],
        scratch_shapes=[
            pltpu.VMEM((total, HD), BF16),
            pltpu.VMEM((total, 2 * HD), BF16),
            pltpu.VMEM((slots, total), F32),
            pltpu.VMEM(w_cond.shape, BF16),
            pltpu.SemaphoreType.DMA,
        ],
        compiler_params=params(),
        name="masked_rows",
    )(arrived, slot_columns, rank_row, in_hbm(w_cond))


def attend_kernel(first, got_ref, qrank_ref, rank_ref, *rest):
    out_ref, key_scr, val_scr, score_scr = rest[-4:]

    @pl.when(pl.program_id(0) == 0)
    def _():
        load_keys(got_ref, key_scr, val_scr)

    source = pl.program_id(0) + first
    columns = qrank_ref[...]
    lanes = lax.broadcasted_iota(jnp.int32, columns.shape, 1)
    ranks = jnp.sum(jnp.where(lanes == source, columns, 0), axis=1, keepdims=True)
    out = attend(got_ref[source, 0], ranks, rank_ref, key_scr, val_scr, score_scr)
    out_ref[0] = out.astype(BF16)


def attend_some(arrived, rank_columns, rank_row, first, count, after, earlier=None):
    heads, _, each, _ = arrived.shape
    total = heads * each
    specs = [
        vmem(),
        vmem(),
        vmem(),
        anywhere(),
    ]
    operands = [arrived, rank_columns, rank_row, after]
    aliases = {}
    if earlier is not None:
        specs.append(anywhere())
        operands.append(earlier)
        aliases = {len(operands) - 1: 0}
    return pl.pallas_call(
        functools.partial(attend_kernel, first),
        grid=(count,),
        in_specs=specs,
        out_specs=pl.BlockSpec((1, each, HD), lambda i: (i + first, 0, 0)),
        out_shape=jax.ShapeDtypeStruct((heads, each + TAIL, HD), BF16),
        scratch_shapes=[
            pltpu.VMEM((total, HD), BF16),
            pltpu.VMEM((total, 2 * HD), BF16),
            pltpu.VMEM((each, total), F32),
        ],
        input_output_aliases=aliases,
        compiler_params=params(),
        name="attention",
    )(*operands)


def head_kernel(
    cond_ref, gain_ref, out_t_ref, noise_ref, feat_ref, base_hbm, after_ref,
    send_ref, token_ref, block_scr, base_ref, sem,
):
    fetch = pltpu.make_async_copy(base_hbm, base_ref, sem)
    fetch.start()
    heads, rows, width = cond_ref.shape
    count = base_ref.shape[0]
    condition = cond_ref[0].astype(F32)
    for source in range(1, heads):
        condition = condition + cond_ref[source].astype(F32)
    fetch.wait()
    hidden = base_ref[...] + jnp.concatenate([condition] * (count // rows), axis=0)
    inverse = lax.rsqrt(jnp.mean(hidden * hidden, axis=1, keepdims=True) + NORM_EPS)
    unit = hidden * inverse
    gain = gain_ref[...]
    scaled = unit * gain
    gate = 1.0 / (1.0 + jnp.exp(-scaled))
    active = scaled * gate
    act_hi, act_lo = two_parts(active)
    out_hi, out_lo = two_parts(out_t_ref[...])
    both = dot_rows(jnp.concatenate([act_hi, act_lo], axis=0), out_hi)
    predicted = both[:count] + both[count:] + dot_rows(act_hi, out_lo)
    pred_grad = (predicted - noise_ref[:, :LAT]) * noise_ref[:, LAT : LAT + 1]
    pg_hi, pg_lo = two_parts(pred_grad)
    both = dot(jnp.concatenate([pg_hi, pg_lo], axis=0), out_hi)
    act_grad = both[:count] + both[count:] + dot(pg_hi, out_lo)
    scaled_grad = act_grad * gate * (1.0 + scaled * (1.0 - gate))
    gain_grad = jnp.sum(scaled_grad * unit, axis=0, keepdims=True)
    unit_grad = scaled_grad * gain
    along = jnp.mean(unit_grad * unit, axis=1, keepdims=True)
    hidden_grad = inverse * (unit_grad - unit * along)
    hg_hi, hg_lo = two_parts(hidden_grad)
    feats = feat_ref[...]
    half = feats.shape[0] // 2
    both = dot(feats, hg_hi)
    feat_grad = both[:half] + both[half:] + dot(feats[:half], hg_lo)
    out_grad = dot_over_rows(pg_hi, act_hi) + dot_over_rows(pg_lo, act_hi)
    out_grad = out_grad + dot_over_rows(pg_hi, act_lo)
    token_ref[...] = inverse[:8] + jnp.zeros(token_ref.shape, F32)
    cond_grad = hidden_grad[:rows]
    for draw in range(1, count // rows):
        cond_grad = cond_grad + hidden_grad[draw * rows : (draw + 1) * rows]
    block_scr[:, :width] = cond_grad
    block_scr[:, width:] = jnp.zeros((rows, EXTRA), F32)
    pieces = width // EXTRA
    for target in range(heads):
        source_rows = feat_grad if 2 * target < LAT else out_grad
        begin = 2 * target % LAT
        block_scr[rows - 2 : rows, :width] = source_rows[begin : begin + 2]
        if target < pieces:
            cols = slice(target * EXTRA, (target + 1) * EXTRA)
            block_scr[0:1, width:] = feat_grad[LAT : LAT + 1, cols]
            block_scr[1:2, width:] = gain_grad[:, cols]
        elif target == pieces:
            block_scr[:, width:] = jnp.zeros((rows, EXTRA), F32)
        send_ref[target] = block_scr[...].astype(BF16)


def grad_kernel(got_ref, picked_ref, after_ref, send_ref, pack_scr):
    heads, rows, wide = got_ref.shape
    width = wide - EXTRA
    groups = send_ref.shape[0]
    cond_grad = got_ref[:, :, :width].reshape(heads * rows, width)
    part = lax.dot_general(
        picked_ref[...], cond_grad, (((0,), (0,)), ((), ())), preferred_element_type=F32
    ).astype(BF16)
    summed = got_ref[0].astype(F32)
    for source in range(1, heads):
        summed = summed + got_ref[source].astype(F32)
    pack_scr[...] = jnp.zeros(pack_scr.shape, F32)
    pieces = width // 128
    for piece in range(pieces):
        row, lane = 2 * (piece % 8), 128 * (piece // 8)
        pack_scr[row : row + 2, lane : lane + 128] = summed[
            rows - 2 : rows, piece * 128 : (piece + 1) * 128
        ]
    row, lane = 2 * (pieces % 8), 128 * (pieces // 8)
    pack_scr[row : row + 2, lane : lane + 128] = summed[0:2, width:]
    packed = pack_scr[...].astype(BF16)
    row_groups = HD // GROUP_ROWS
    col_groups = groups // row_groups
    cols = width // col_groups
    for group in range(groups):
        top = group // col_groups * GROUP_ROWS
        left = group % col_groups * cols
        send_ref[group, :, :cols] = part[top : top + GROUP_ROWS, left : left + cols]
        send_ref[group, :, cols:] = packed


def total_kernel(got_ref, attended_ref, big_ref, tail_ref):
    groups, rows, wide = got_ref.shape
    cols = wide - PACK
    total = got_ref[0].astype(F32)
    for source in range(1, groups):
        total = total + got_ref[source].astype(F32)
    rounded = total.astype(BF16)
    big_ref[...] = rounded[:, :cols]
    for head in range(tail_ref.shape[0]):
        tail_ref[head, :rows] = rounded[:, cols : cols + HD]
        tail_ref[head, rows:] = rounded[:, cols + HD :]


def total_over_clips(got, attended, each):
    groups, rows, wide = got.shape
    heads = attended.shape[0]
    return pl.pallas_call(
        total_kernel,
        grid=(1,),
        in_specs=[vmem(), anywhere()],
        out_specs=[vmem(), pl.BlockSpec((heads, TAIL, HD), lambda i: (0, each // TAIL, 0))],
        out_shape=[
            jax.ShapeDtypeStruct((rows, wide - PACK), BF16),
            jax.ShapeDtypeStruct(attended.shape, BF16),
        ],
        input_output_aliases={1: 1},
        compiler_params=params(),
        name="sum_over_clips",
    )(got, attended)


def spread_kernel(big_ref, tail_ref, cond_ref, in_ref, time_ref, gain_ref, out_ref):
    groups, rows, cols = big_ref.shape
    heads = tail_ref.shape[0]
    width = cond_ref.shape[1]
    col_groups = width // cols
    for group in range(groups):
        top = group // col_groups * GROUP_ROWS
        left = group % col_groups * cols
        cond_ref[top : top + GROUP_ROWS, left : left + cols] = big_ref[group].astype(F32)
    pieces = width // 128
    for head in range(heads):
        packed = tail_ref[head].astype(F32)
        target = in_ref if 2 * head < LAT else out_ref
        begin = 2 * head % LAT
        for piece in range(pieces):
            row = 2 * (piece % 8) + GROUP_ROWS * (piece // 8)
            target[begin : begin + 2, piece * 128 : (piece + 1) * 128] = packed[row : row + 2]
        if head < pieces:
            row = 2 * (pieces % 8) + GROUP_ROWS * (pieces // 8)
            cut = slice(head * 128, (head + 1) * 128)
            time_ref[cut] = packed[row]
            gain_ref[cut] = packed[row + 1]


def write_gradients(big, returned, each, width):
    heads = returned.shape[0]
    return pl.pallas_call(
        spread_kernel,
        grid=(1,),
        in_specs=[
            vmem(),
            pl.BlockSpec((heads, TAIL, HD), lambda i: (0, each // TAIL, 0)),
        ],
        out_specs=[vmem()] * 5,
        out_shape=[
            jax.ShapeDtypeStruct((HD, width), F32),
            jax.ShapeDtypeStruct((LAT, width), F32),
            jax.ShapeDtypeStruct((width,), F32),
            jax.ShapeDtypeStruct((width,), F32),
            jax.ShapeDtypeStruct((LAT, width), F32),
        ],
        compiler_params=params(),
        name="write_gradients",
    )(big, returned)


def call(kernel, out_shape, scratch, name, *operands, outside=0):
    specs = [vmem()] * (len(operands) - outside) + [anywhere()] * outside
    many = isinstance(out_shape, list)
    return pl.pallas_call(
        kernel,
        in_specs=specs,
        out_specs=[vmem()] * len(out_shape) if many else vmem(),
        out_shape=out_shape,
        scratch_shapes=scratch,
        compiler_params=params(),
        name=name,
    )(*operands)


def exchange(value, axis):
    return lax.all_to_all(value, axis, split_axis=0, concat_axis=0, tiled=True)


def local(
    queries, key_rows, value_rows, token_rank, masked_index, masked_counts, clean_latents,
    noise_draws, noise_times, w_cond, w_in, time_vec, norm_gain, w_out,
):
    each = queries.shape[0]
    heads = lax.axis_size("head")
    groups = lax.axis_size("seq")
    total = each * heads
    width = w_cond.shape[1]
    share = masked_index.shape[1] // heads
    count = DRAWS * SLOT

    stacked = stack_by_head(queries, key_rows, value_rows, heads)
    arrived = in_vmem(exchange(stacked, "head"))

    chosen = masked_index[0]
    live = lax.dynamic_index_in_dim(masked_counts, lax.axis_index("seq"), 0, keepdims=False)
    alive = jnp.arange(heads * share, dtype=jnp.int32) < live
    ranks = token_rank[0]

    def in_slots(value, fill):
        value = value.reshape(heads, share)
        return jnp.pad(value, ((0, 0), (0, SLOT - share)), constant_values=fill)

    where = in_slots(jnp.where(alive, chosen, -1), -1).reshape(heads * SLOT)
    where_rank = in_slots(jnp.where(alive, jnp.take(ranks, chosen), -1), -1)
    slot_columns = jnp.stack([where, where_rank.reshape(heads * SLOT)], axis=1)
    rank_row = ranks.reshape(1, total)
    rank_columns = jnp.pad(ranks.reshape(heads, each).T, ((0, 0), (0, 128 - heads)))

    mine = lax.dynamic_index_in_dim(
        in_slots(chosen, 0), lax.axis_index("head"), 0, keepdims=False
    )
    my_alive = lax.dynamic_index_in_dim(
        in_slots(alive.astype(F32), 0.0), lax.axis_index("head"), 0, keepdims=False
    )
    clean = jnp.take(clean_latents, mine, axis=0).astype(F32)
    noise = jnp.take(noise_draws, mine, axis=0).astype(F32)
    times = jnp.take(noise_times, mine, axis=0).astype(F32)
    noise = jnp.transpose(noise.reshape(SLOT, DRAWS, LAT), (1, 0, 2))
    times = jnp.transpose(times)[:, :, None]
    angles = 0.5 * math.pi * times
    noisy = (jnp.cos(angles) * clean[None] + jnp.sin(angles) * noise).reshape(count, LAT)
    times = times.reshape(count, 1)
    noise = noise.reshape(count, LAT)
    base = jnp.dot(noisy, w_in, precision=lax.Precision.HIGHEST) + times * time_vec
    loss_scale = 1.0 / math.sqrt(masked_index.shape[1] // 3 * groups * DRAWS)
    row_weight = jnp.tile(my_alive * (2.0 * loss_scale), DRAWS).reshape(count, 1)
    feats = jnp.pad(jnp.concatenate([noisy, times], axis=1), ((0, 0), (0, 15))).T
    feats = jnp.concatenate(two_parts(feats), axis=0)

    gain = norm_gain.reshape(1, width)
    noise = jnp.concatenate([noise, row_weight], axis=1)
    slot_columns, rank_columns, base, gain, noise, feats = lax.optimization_barrier(
        (slot_columns, rank_columns, base, gain, noise, feats)
    )
    part, picked = attend_masked(arrived, slot_columns, rank_row, w_cond)
    half = heads // 2
    got_cond = exchange(part, "head")
    first_half = attend_some(arrived, rank_columns, rank_row, 0, half, picked)

    send, token = call(
        head_kernel,
        [
            pltpu.HBM((heads, SLOT, width + EXTRA), BF16),
            jax.ShapeDtypeStruct((8, 128), F32),
        ],
        [
            pltpu.VMEM((SLOT, width + EXTRA), F32),
            pltpu.VMEM(base.shape, F32),
            pltpu.SemaphoreType.DMA,
        ],
        "diffusion_head",
        in_vmem(got_cond), gain, w_out.T, noise, feats, in_hbm(base), first_half,
        outside=2,
    )
    got_grad = exchange(send, "head")
    attended = attend_some(arrived, rank_columns, rank_row, half, half, token, first_half)

    col_groups = groups // (HD // GROUP_ROWS)
    cols = width // col_groups
    parts = call(
        grad_kernel,
        jax.ShapeDtypeStruct((groups, GROUP_ROWS, cols + PACK), BF16),
        [pltpu.VMEM((GROUP_ROWS, PACK), F32)],
        "cond_weight_grad",
        in_vmem(got_grad), picked, attended,
        outside=1,
    )
    got_parts = exchange(parts, "seq")
    big, message = total_over_clips(in_vmem(got_parts), attended, each)
    returned = exchange(message, "head")
    all_big = lax.all_gather(big, "seq")
    cond_whole, in_grad, time_grad, gain_grad, out_grad = write_gradients(
        all_big, returned, each, width
    )
    rows = jnp.transpose(returned[:, :each], (1, 0, 2)).reshape(each, heads * HD)
    return (rows, cond_whole, in_grad, time_grad, gain_grad, out_grad.T)


def solution(mesh):
    return jax.shard_map(
        local,
        mesh=mesh,
        in_specs=(
            P(("seq", "head"), None),
            P(("seq", "head"), None),
            P(("seq", "head"), None),
            P("seq", None),
            P("seq", None),
            P(),
            P("seq", None),
            P("seq", None),
            P("seq", None),
            P("head", None),
            P(),
            P(),
            P(),
            P(),
        ),
        out_specs=(P(("seq", "head"), None), P("head", None), P(), P(), P(), P()),
        check_vma=False,
    )
```

```python
import functools
import math

import jax
import jax.numpy as jnp
from jax import lax
from jax.experimental import pallas as pl
from jax.experimental.pallas import tpu as pltpu
from jax.sharding import PartitionSpec as P

HD = 128
LAT = 16
DRAWS = 4
NORM_EPS = 1e-06
HIDDEN_SCORE = -1e30
SLOT = 16
EXTRA = 128
PACK = 256
TAIL = 32
GROUP_ROWS = 16
STAGES = ((8, 16, 24), (4, 2, 6), (1,))
LOG2E = 1.4426950408889634
F32 = jnp.float32
BF16 = jnp.bfloat16
VMEM_LIMIT = 32 * 1024 * 1024


def params():
    return pltpu.CompilerParams(vmem_limit_bytes=VMEM_LIMIT)


def vmem():
    return pl.BlockSpec(memory_space=pltpu.VMEM)


def anywhere():
    return pl.BlockSpec(memory_space=pl.ANY)


def dot(a, b):
    return jnp.dot(a, b, preferred_element_type=F32)


def dot_rows(a, b):
    return lax.dot_general(a, b, (((1,), (1,)), ((), ())), preferred_element_type=F32)


def dot_over_rows(a, b):
    return lax.dot_general(a, b, (((0,), (0,)), ((), ())), preferred_element_type=F32)


def two_parts(value):
    high = value.astype(BF16)
    return high, (value - high.astype(F32)).astype(BF16)


def in_vmem(value):
    return pltpu.with_memory_space_constraint(value, pltpu.VMEM)


def in_hbm(value):
    return pltpu.with_memory_space_constraint(value, pltpu.HBM)


def stack_kernel(q_ref, k_ref, v_ref, out_ref):
    for head in range(out_ref.shape[0]):
        cols = slice(head * HD, (head + 1) * HD)
        out_ref[head, 0] = q_ref[:, cols]
        out_ref[head, 1] = k_ref[:, cols]
        out_ref[head, 2] = v_ref[:, cols]


def stack_by_head(queries, key_rows, value_rows, heads):
    each = queries.shape[0]
    block = each // 2
    spec = pl.BlockSpec((block, heads * HD), lambda i: (i, 0))
    return pl.pallas_call(
        stack_kernel,
        grid=(2,),
        in_specs=[spec, spec, spec],
        out_specs=pl.BlockSpec((heads, 3, block, HD), lambda i: (0, 0, i, 0)),
        out_shape=pltpu.HBM((heads, 3, each, HD), BF16),
        compiler_params=params(),
        name="stack_by_head",
    )(in_hbm(queries), in_hbm(key_rows), in_hbm(value_rows))


def load_keys(got_ref, key_scr, val_scr):
    rows = key_scr.shape[0]
    key_scr[...] = got_ref[:, 1].reshape(rows, HD)
    val_scr[:, :HD] = got_ref[:, 2].reshape(rows, HD)
    val_scr[:, HD:] = jnp.ones((rows, HD), BF16)


def attend(query, query_rank, rank_ref, key_scr, val_scr, score_scr):
    total = key_scr.shape[0]
    chunk = math.gcd(total, 512)
    scale = LOG2E / math.sqrt(HD)
    top = None
    for start in range(0, total, chunk):
        scores = lax.dot_general(
            query,
            key_scr[start : start + chunk, :],
            (((1,), (1,)), ((), ())),
            preferred_element_type=F32,
        )
        visible = rank_ref[:, start : start + chunk] <= query_rank
        scores = jnp.where(visible, scores, HIDDEN_SCORE)
        score_scr[:, start : start + chunk] = scores
        for lane in range(0, chunk, 128):
            part = scores[:, lane : lane + 128]
            top = part if top is None else jnp.maximum(top, part)
    top = jnp.max(top, axis=1, keepdims=True)
    total_out = None
    for start in range(0, total, chunk):
        weights = jnp.exp2((score_scr[:, start : start + chunk] - top) * scale)
        mixed = dot(weights.astype(BF16), val_scr[start : start + chunk, :])
        total_out = mixed if total_out is None else total_out + mixed
    return total_out[:, :HD] / total_out[:, HD:]


def masked_kernel(got_ref, slot_ref, rank_ref, w_ref, *rest):
    part_ref, picked_ref, key_scr, val_scr, score_scr, w_scr, sem = rest
    fetch = pltpu.make_async_copy(w_ref, w_scr, sem)
    fetch.start()
    load_keys(got_ref, key_scr, val_scr)
    slots = slot_ref.shape[0]
    where = slot_ref[:, 0:1]
    slot_rank = slot_ref[:, 1:2]
    total = key_scr.shape[0]
    sources, _, each, _ = got_ref.shape
    query = jnp.zeros((slots, HD), F32)
    step = math.gcd(each * sources, each * 4)
    for start in range(0, total, step):
        lanes = lax.broadcasted_iota(jnp.int32, (slots, step), 1) + start
        hit = jnp.where(lanes == where, 1.0, 0.0).astype(BF16)
        rows = got_ref[start // each : (start + step) // each, 0].reshape(step, HD)
        query = query + dot(hit, rows)
    out = attend(query.astype(BF16), slot_rank, rank_ref, key_scr, val_scr, score_scr)
    picked = jnp.where(slot_rank >= 0, out, 0.0).astype(BF16)
    picked_ref[...] = picked
    fetch.wait()
    part = dot(picked, w_scr[...]).astype(BF16)
    part_ref[...] = part.reshape(part_ref.shape)


def attend_masked(arrived, slot_columns, rank_row, w_cond):
    heads, _, each, _ = arrived.shape
    total = heads * each
    slots = slot_columns.shape[0]
    width = w_cond.shape[1]
    return pl.pallas_call(
        masked_kernel,
        in_specs=[vmem()] * 3 + [anywhere()],
        out_specs=[vmem(), vmem()],
        out_shape=[
            pltpu.HBM((heads, slots // heads, width), BF16),
            jax.ShapeDtypeStruct((slots, HD), BF16),
        ],
        scratch_shapes=[
            pltpu.VMEM((total, HD), BF16),
            pltpu.VMEM((total, 2 * HD), BF16),
            pltpu.VMEM((slots, total), F32),
            pltpu.VMEM(w_cond.shape, BF16),
            pltpu.SemaphoreType.DMA,
        ],
        compiler_params=params(),
        name="masked_rows",
    )(arrived, slot_columns, rank_row, in_hbm(w_cond))


def attend_kernel(first, got_ref, qrank_ref, rank_ref, *rest):
    out_ref, key_scr, val_scr, score_scr = rest[-4:]

    @pl.when(pl.program_id(0) == 0)
    def _():
        load_keys(got_ref, key_scr, val_scr)

    source = pl.program_id(0) + first
    columns = qrank_ref[...]
    lanes = lax.broadcasted_iota(jnp.int32, columns.shape, 1)
    ranks = jnp.sum(jnp.where(lanes == source, columns, 0), axis=1, keepdims=True)
    out = attend(got_ref[source, 0], ranks, rank_ref, key_scr, val_scr, score_scr)
    out_ref[0] = out.astype(BF16)


def attend_some(arrived, rank_columns, rank_row, first, count, after, earlier=None):
    heads, _, each, _ = arrived.shape
    total = heads * each
    specs = [
        vmem(),
        vmem(),
        vmem(),
        anywhere(),
    ]
    operands = [arrived, rank_columns, rank_row, after]
    aliases = {}
    if earlier is not None:
        specs.append(anywhere())
        operands.append(earlier)
        aliases = {len(operands) - 1: 0}
    return pl.pallas_call(
        functools.partial(attend_kernel, first),
        grid=(count,),
        in_specs=specs,
        out_specs=pl.BlockSpec((1, each, HD), lambda i: (i + first, 0, 0)),
        out_shape=jax.ShapeDtypeStruct((heads, each + TAIL, HD), BF16),
        scratch_shapes=[
            pltpu.VMEM((total, HD), BF16),
            pltpu.VMEM((total, 2 * HD), BF16),
            pltpu.VMEM((each, total), F32),
        ],
        input_output_aliases=aliases,
        compiler_params=params(),
        name="attention",
    )(*operands)


def head_kernel(
    cond_ref, gain_ref, out_t_ref, noise_ref, feat_ref, base_hbm, after_ref,
    send_ref, token_ref, block_scr, base_ref, sem,
):
    fetch = pltpu.make_async_copy(base_hbm, base_ref, sem)
    fetch.start()
    heads, rows, width = cond_ref.shape
    count = base_ref.shape[0]
    condition = cond_ref[0].astype(F32)
    for source in range(1, heads):
        condition = condition + cond_ref[source].astype(F32)
    fetch.wait()
    hidden = base_ref[...] + jnp.concatenate([condition] * (count // rows), axis=0)
    inverse = lax.rsqrt(jnp.mean(hidden * hidden, axis=1, keepdims=True) + NORM_EPS)
    unit = hidden * inverse
    gain = gain_ref[...]
    scaled = unit * gain
    gate = 1.0 / (1.0 + jnp.exp(-scaled))
    active = scaled * gate
    act_hi, act_lo = two_parts(active)
    out_hi, out_lo = two_parts(out_t_ref[...])
    both = dot_rows(jnp.concatenate([act_hi, act_lo], axis=0), out_hi)
    predicted = both[:count] + both[count:] + dot_rows(act_hi, out_lo)
    pred_grad = (predicted - noise_ref[:, :LAT]) * noise_ref[:, LAT : LAT + 1]
    pg_hi, pg_lo = two_parts(pred_grad)
    both = dot(jnp.concatenate([pg_hi, pg_lo], axis=0), out_hi)
    act_grad = both[:count] + both[count:] + dot(pg_hi, out_lo)
    scaled_grad = act_grad * gate * (1.0 + scaled * (1.0 - gate))
    gain_grad = jnp.sum(scaled_grad * unit, axis=0, keepdims=True)
    unit_grad = scaled_grad * gain
    along = jnp.mean(unit_grad * unit, axis=1, keepdims=True)
    hidden_grad = inverse * (unit_grad - unit * along)
    hg_hi, hg_lo = two_parts(hidden_grad)
    feats = feat_ref[...]
    half = feats.shape[0] // 2
    both = dot(feats, hg_hi)
    feat_grad = both[:half] + both[half:] + dot(feats[:half], hg_lo)
    out_grad = dot_over_rows(pg_hi, act_hi) + dot_over_rows(pg_lo, act_hi)
    out_grad = out_grad + dot_over_rows(pg_hi, act_lo)
    token_ref[...] = inverse[:8] + jnp.zeros(token_ref.shape, F32)
    cond_grad = hidden_grad[:rows]
    for draw in range(1, count // rows):
        cond_grad = cond_grad + hidden_grad[draw * rows : (draw + 1) * rows]
    block_scr[:, :width] = cond_grad
    block_scr[:, width:] = jnp.zeros((rows, EXTRA), F32)
    pieces = width // EXTRA
    for target in range(heads):
        source_rows = feat_grad if 2 * target < LAT else out_grad
        begin = 2 * target % LAT
        block_scr[rows - 2 : rows, :width] = source_rows[begin : begin + 2]
        if target < pieces:
            cols = slice(target * EXTRA, (target + 1) * EXTRA)
            block_scr[0:1, width:] = feat_grad[LAT : LAT + 1, cols]
            block_scr[1:2, width:] = gain_grad[:, cols]
        elif target == pieces:
            block_scr[:, width:] = jnp.zeros((rows, EXTRA), F32)
        send_ref[target] = block_scr[...].astype(BF16)


def grad_kernel(got_ref, picked_ref, after_ref, send_ref, pack_scr):
    heads, rows, wide = got_ref.shape
    width = wide - EXTRA
    groups = send_ref.shape[0]
    cond_grad = got_ref[:, :, :width].reshape(heads * rows, width)
    part = lax.dot_general(
        picked_ref[...], cond_grad, (((0,), (0,)), ((), ())), preferred_element_type=F32
    ).astype(BF16)
    summed = got_ref[0].astype(F32)
    for source in range(1, heads):
        summed = summed + got_ref[source].astype(F32)
    pack_scr[...] = jnp.zeros(pack_scr.shape, F32)
    pieces = width // 128
    for piece in range(pieces):
        row, lane = 2 * (piece % 8), 128 * (piece // 8)
        pack_scr[row : row + 2, lane : lane + 128] = summed[
            rows - 2 : rows, piece * 128 : (piece + 1) * 128
        ]
    row, lane = 2 * (pieces % 8), 128 * (pieces // 8)
    pack_scr[row : row + 2, lane : lane + 128] = summed[0:2, width:]
    packed = pack_scr[...].astype(BF16)
    row_groups = HD // GROUP_ROWS
    col_groups = groups // row_groups
    cols = width // col_groups
    for group in range(groups):
        top = group // col_groups * GROUP_ROWS
        left = group % col_groups * cols
        send_ref[group, :, :cols] = part[top : top + GROUP_ROWS, left : left + cols]
        send_ref[group, :, cols:] = packed


def total_kernel(got_ref, attended_ref, big_ref, tail_ref):
    groups, rows, wide = got_ref.shape
    cols = wide - PACK
    total = got_ref[0].astype(F32)
    for source in range(1, groups):
        total = total + got_ref[source].astype(F32)
    rounded = total.astype(BF16)
    big_ref[...] = rounded[:, :cols]
    for head in range(tail_ref.shape[0]):
        tail_ref[head, :rows] = rounded[:, cols : cols + HD]
        tail_ref[head, rows:] = rounded[:, cols + HD :]


def total_over_clips(got, attended, each):
    groups, rows, wide = got.shape
    heads = attended.shape[0]
    return pl.pallas_call(
        total_kernel,
        grid=(1,),
        in_specs=[vmem(), anywhere()],
        out_specs=[vmem(), pl.BlockSpec((heads, TAIL, HD), lambda i: (0, each // TAIL, 0))],
        out_shape=[
            jax.ShapeDtypeStruct((rows, wide - PACK), BF16),
            jax.ShapeDtypeStruct(attended.shape, BF16),
        ],
        input_output_aliases={1: 1},
        compiler_params=params(),
        name="sum_over_clips",
    )(got, attended)


def spread_kernel(order, seq_ref, *refs):
    tail_ref, cond_ref, in_ref, time_ref, gain_ref, out_ref = refs[-6:]
    cols = refs[0].shape[2]
    heads = tail_ref.shape[0]
    width = cond_ref.shape[1]
    col_groups = width // cols
    seq = seq_ref[0]
    for big_ref, masks in zip(refs, order):
        for place, mask in enumerate(masks):
            group = seq ^ mask
            top = pl.multiple_of(group // col_groups * GROUP_ROWS, GROUP_ROWS)
            left = pl.multiple_of(lax.rem(group, col_groups) * cols, 128)
            cond_ref[pl.ds(top, GROUP_ROWS), pl.ds(left, cols)] = big_ref[place].astype(F32)
    pieces = width // 128
    for head in range(heads):
        packed = tail_ref[head].astype(F32)
        target = in_ref if 2 * head < LAT else out_ref
        begin = 2 * head % LAT
        for piece in range(pieces):
            row = 2 * (piece % 8) + GROUP_ROWS * (piece // 8)
            target[begin : begin + 2, piece * 128 : (piece + 1) * 128] = packed[row : row + 2]
        if head < pieces:
            row = 2 * (pieces % 8) + GROUP_ROWS * (pieces // 8)
            cut = slice(head * 128, (head + 1) * 128)
            time_ref[cut] = packed[row]
            gain_ref[cut] = packed[row + 1]


def write_gradients(seq, big, order, returned, each, width):
    heads = returned.shape[0]
    return pl.pallas_call(
        functools.partial(spread_kernel, order),
        grid=(1,),
        in_specs=[
            pl.BlockSpec(memory_space=pltpu.SMEM),
            *[vmem()] * len(big),
            pl.BlockSpec((heads, TAIL, HD), lambda i: (0, each // TAIL, 0)),
        ],
        out_specs=[vmem()] * 5,
        out_shape=[
            jax.ShapeDtypeStruct((HD, width), F32),
            jax.ShapeDtypeStruct((LAT, width), F32),
            jax.ShapeDtypeStruct((width,), F32),
            jax.ShapeDtypeStruct((width,), F32),
            jax.ShapeDtypeStruct((LAT, width), F32),
        ],
        compiler_params=params(),
        name="write_gradients",
    )(seq, *big, returned)


def call(kernel, out_shape, scratch, name, *operands, outside=0):
    specs = [vmem()] * (len(operands) - outside) + [anywhere()] * outside
    many = isinstance(out_shape, list)
    return pl.pallas_call(
        kernel,
        in_specs=specs,
        out_specs=[vmem()] * len(out_shape) if many else vmem(),
        out_shape=out_shape,
        scratch_shapes=scratch,
        compiler_params=params(),
        name=name,
    )(*operands)


def gather_over_clips(piece, groups):
    parts, order = [piece[None]], [[0]]
    for stage in STAGES:
        held = parts[0] if len(parts) == 1 else jnp.concatenate(parts)
        masks = [mask for part in order for mask in part]
        parts, order = [held], [masks]
        for partner in stage:
            if partner < groups:
                pairs = [(source, source ^ partner) for source in range(groups)]
                parts.append(lax.ppermute(held, "seq", pairs))
                order.append([mask ^ partner for mask in masks])
    return parts, order


def exchange(value, axis):
    return lax.all_to_all(value, axis, split_axis=0, concat_axis=0, tiled=True)


def local(
    queries, key_rows, value_rows, token_rank, masked_index, masked_counts, clean_latents,
    noise_draws, noise_times, w_cond, w_in, time_vec, norm_gain, w_out,
):
    each = queries.shape[0]
    heads = lax.axis_size("head")
    groups = lax.axis_size("seq")
    total = each * heads
    width = w_cond.shape[1]
    share = masked_index.shape[1] // heads
    count = DRAWS * SLOT

    stacked = stack_by_head(queries, key_rows, value_rows, heads)
    arrived = in_vmem(exchange(stacked, "head"))

    chosen = masked_index[0]
    live = lax.dynamic_index_in_dim(masked_counts, lax.axis_index("seq"), 0, keepdims=False)
    alive = jnp.arange(heads * share, dtype=jnp.int32) < live
    ranks = token_rank[0]

    def in_slots(value, fill):
        value = value.reshape(heads, share)
        return jnp.pad(value, ((0, 0), (0, SLOT - share)), constant_values=fill)

    where = in_slots(jnp.where(alive, chosen, -1), -1).reshape(heads * SLOT)
    where_rank = in_slots(jnp.where(alive, jnp.take(ranks, chosen), -1), -1)
    slot_columns = jnp.stack([where, where_rank.reshape(heads * SLOT)], axis=1)
    rank_row = ranks.reshape(1, total)
    rank_columns = jnp.pad(ranks.reshape(heads, each).T, ((0, 0), (0, 128 - heads)))

    mine = lax.dynamic_index_in_dim(
        in_slots(chosen, 0), lax.axis_index("head"), 0, keepdims=False
    )
    my_alive = lax.dynamic_index_in_dim(
        in_slots(alive.astype(F32), 0.0), lax.axis_index("head"), 0, keepdims=False
    )
    clean = jnp.take(clean_latents, mine, axis=0).astype(F32)
    noise = jnp.take(noise_draws, mine, axis=0).astype(F32)
    times = jnp.take(noise_times, mine, axis=0).astype(F32)
    noise = jnp.transpose(noise.reshape(SLOT, DRAWS, LAT), (1, 0, 2))
    times = jnp.transpose(times)[:, :, None]
    angles = 0.5 * math.pi * times
    noisy = (jnp.cos(angles) * clean[None] + jnp.sin(angles) * noise).reshape(count, LAT)
    times = times.reshape(count, 1)
    noise = noise.reshape(count, LAT)
    base = jnp.dot(noisy, w_in, precision=lax.Precision.HIGHEST) + times * time_vec
    loss_scale = 1.0 / math.sqrt(masked_index.shape[1] // 3 * groups * DRAWS)
    row_weight = jnp.tile(my_alive * (2.0 * loss_scale), DRAWS).reshape(count, 1)
    feats = jnp.pad(jnp.concatenate([noisy, times], axis=1), ((0, 0), (0, 15))).T
    feats = jnp.concatenate(two_parts(feats), axis=0)

    gain = norm_gain.reshape(1, width)
    noise = jnp.concatenate([noise, row_weight], axis=1)
    slot_columns, rank_columns, base, gain, noise, feats = lax.optimization_barrier(
        (slot_columns, rank_columns, base, gain, noise, feats)
    )
    part, picked = attend_masked(arrived, slot_columns, rank_row, w_cond)
    half = heads // 2
    got_cond = exchange(part, "head")
    first_half = attend_some(arrived, rank_columns, rank_row, 0, half, picked)

    send, token = call(
        head_kernel,
        [
            pltpu.HBM((heads, SLOT, width + EXTRA), BF16),
            jax.ShapeDtypeStruct((8, 128), F32),
        ],
        [
            pltpu.VMEM((SLOT, width + EXTRA), F32),
            pltpu.VMEM(base.shape, F32),
            pltpu.SemaphoreType.DMA,
        ],
        "diffusion_head",
        in_vmem(got_cond), gain, w_out.T, noise, feats, in_hbm(base), first_half,
        outside=2,
    )
    got_grad = exchange(send, "head")
    attended = attend_some(arrived, rank_columns, rank_row, half, half, token, first_half)

    col_groups = groups // (HD // GROUP_ROWS)
    cols = width // col_groups
    parts = call(
        grad_kernel,
        jax.ShapeDtypeStruct((groups, GROUP_ROWS, cols + PACK), BF16),
        [pltpu.VMEM((GROUP_ROWS, PACK), F32)],
        "cond_weight_grad",
        in_vmem(got_grad), picked, attended,
        outside=1,
    )
    got_parts = exchange(parts, "seq")
    big, message = total_over_clips(in_vmem(got_parts), attended, each)
    returned = exchange(message, "head")
    all_big, order = gather_over_clips(big, groups)
    cond_whole, in_grad, time_grad, gain_grad, out_grad = write_gradients(
        lax.axis_index("seq").reshape(1), all_big, order, returned, each, width
    )
    rows = jnp.transpose(returned[:, :each], (1, 0, 2)).reshape(each, heads * HD)
    return (rows, cond_whole, in_grad, time_grad, gain_grad, out_grad.T)


def solution(mesh):
    return jax.shard_map(
        local,
        mesh=mesh,
        in_specs=(
            P(("seq", "head"), None),
            P(("seq", "head"), None),
            P(("seq", "head"), None),
            P("seq", None),
            P("seq", None),
            P(),
            P("seq", None),
            P("seq", None),
            P("seq", None),
            P("head", None),
            P(),
            P(),
            P(),
            P(),
        ),
        out_specs=(P(("seq", "head"), None), P("head", None), P(), P(), P(), P()),
        check_vma=False,
    )
```

```python
import functools
import math

import jax
import jax.numpy as jnp
from jax import lax
from jax.experimental import pallas as pl
from jax.experimental.pallas import tpu as pltpu
from jax.sharding import PartitionSpec as P

HD = 128
LAT = 16
DRAWS = 4
NORM_EPS = 1e-06
HIDDEN_SCORE = -1e30
SLOT = 16
EARLY = 6
EXTRA = 128
PACK = 256
TAIL = 32
GROUP_ROWS = 16
LOG2E = 1.4426950408889634
F32 = jnp.float32
BF16 = jnp.bfloat16
VMEM_LIMIT = 32 * 1024 * 1024


def params():
    return pltpu.CompilerParams(vmem_limit_bytes=VMEM_LIMIT)


def vmem():
    return pl.BlockSpec(memory_space=pltpu.VMEM)


def anywhere():
    return pl.BlockSpec(memory_space=pl.ANY)


def dot(a, b):
    return jnp.dot(a, b, preferred_element_type=F32)


def dot_rows(a, b):
    return lax.dot_general(a, b, (((1,), (1,)), ((), ())), preferred_element_type=F32)


def dot_over_rows(a, b):
    return lax.dot_general(a, b, (((0,), (0,)), ((), ())), preferred_element_type=F32)


def two_parts(value):
    high = value.astype(BF16)
    return high, (value - high.astype(F32)).astype(BF16)


def in_vmem(value):
    return pltpu.with_memory_space_constraint(value, pltpu.VMEM)


def in_hbm(value):
    return pltpu.with_memory_space_constraint(value, pltpu.HBM)


def stack_kernel(q_ref, k_ref, v_ref, out_ref):
    for head in range(out_ref.shape[0]):
        cols = slice(head * HD, (head + 1) * HD)
        out_ref[head, 0] = q_ref[:, cols]
        out_ref[head, 1] = k_ref[:, cols]
        out_ref[head, 2] = v_ref[:, cols]


def stack_by_head(queries, key_rows, value_rows, heads):
    each = queries.shape[0]
    block = each // 2
    spec = pl.BlockSpec((block, heads * HD), lambda i: (i, 0))
    return pl.pallas_call(
        stack_kernel,
        grid=(2,),
        in_specs=[spec, spec, spec],
        out_specs=pl.BlockSpec((heads, 3, block, HD), lambda i: (0, 0, i, 0)),
        out_shape=pltpu.HBM((heads, 3, each, HD), BF16),
        compiler_params=params(),
        name="stack_by_head",
    )(in_hbm(queries), in_hbm(key_rows), in_hbm(value_rows))


def load_keys(got_ref, key_scr, val_scr):
    rows = key_scr.shape[0]
    key_scr[...] = got_ref[:, 1].reshape(rows, HD)
    val_scr[:, :HD] = got_ref[:, 2].reshape(rows, HD)
    val_scr[:, HD:] = jnp.ones((rows, HD), BF16)


def attend(query, query_rank, rank_ref, key_scr, val_scr, score_scr):
    total = key_scr.shape[0]
    chunk = math.gcd(total, 512)
    scale = LOG2E / math.sqrt(HD)
    top = None
    for start in range(0, total, chunk):
        scores = lax.dot_general(
            query,
            key_scr[start : start + chunk, :],
            (((1,), (1,)), ((), ())),
            preferred_element_type=F32,
        )
        visible = rank_ref[:, start : start + chunk] <= query_rank
        scores = jnp.where(visible, scores, HIDDEN_SCORE)
        score_scr[:, start : start + chunk] = scores
        for lane in range(0, chunk, 128):
            part = scores[:, lane : lane + 128]
            top = part if top is None else jnp.maximum(top, part)
    top = jnp.max(top, axis=1, keepdims=True)
    total_out = None
    for start in range(0, total, chunk):
        weights = jnp.exp2((score_scr[:, start : start + chunk] - top) * scale)
        mixed = dot(weights.astype(BF16), val_scr[start : start + chunk, :])
        total_out = mixed if total_out is None else total_out + mixed
    return total_out[:, :HD] / total_out[:, HD:]


def masked_kernel(got_ref, slot_ref, rank_ref, w_ref, *rest):
    part_ref, picked_ref, key_scr, val_scr, score_scr, w_scr, sem = rest
    fetch = pltpu.make_async_copy(w_ref, w_scr, sem)
    fetch.start()
    load_keys(got_ref, key_scr, val_scr)
    slots = slot_ref.shape[0]
    where = slot_ref[:, 0:1]
    slot_rank = slot_ref[:, 1:2]
    total = key_scr.shape[0]
    sources, _, each, _ = got_ref.shape
    query = jnp.zeros((slots, HD), F32)
    step = math.gcd(each * sources, each * 4)
    for start in range(0, total, step):
        lanes = lax.broadcasted_iota(jnp.int32, (slots, step), 1) + start
        hit = jnp.where(lanes == where, 1.0, 0.0).astype(BF16)
        rows = got_ref[start // each : (start + step) // each, 0].reshape(step, HD)
        query = query + dot(hit, rows)
    out = attend(query.astype(BF16), slot_rank, rank_ref, key_scr, val_scr, score_scr)
    picked = jnp.where(slot_rank >= 0, out, 0.0).astype(BF16)
    picked_ref[...] = picked
    fetch.wait()
    part = dot(picked, w_scr[...]).astype(BF16)
    part_ref[...] = part.reshape(part_ref.shape)


def attend_masked(arrived, slot_columns, rank_row, w_cond):
    heads, _, each, _ = arrived.shape
    total = heads * each
    slots = slot_columns.shape[0]
    width = w_cond.shape[1]
    return pl.pallas_call(
        masked_kernel,
        in_specs=[vmem()] * 3 + [anywhere()],
        out_specs=[vmem(), vmem()],
        out_shape=[
            pltpu.HBM((heads, slots // heads, width), BF16),
            jax.ShapeDtypeStruct((slots, HD), BF16),
        ],
        scratch_shapes=[
            pltpu.VMEM((total, HD), BF16),
            pltpu.VMEM((total, 2 * HD), BF16),
            pltpu.VMEM((slots, total), F32),
            pltpu.VMEM(w_cond.shape, BF16),
            pltpu.SemaphoreType.DMA,
        ],
        compiler_params=params(),
        name="masked_rows",
    )(arrived, slot_columns, rank_row, in_hbm(w_cond))


def attend_kernel(first, got_ref, qrank_ref, rank_ref, *rest):
    out_ref, key_scr, val_scr, score_scr = rest[-4:]

    @pl.when(pl.program_id(0) == 0)
    def _():
        load_keys(got_ref, key_scr, val_scr)

    source = pl.program_id(0) + first
    columns = qrank_ref[...]
    lanes = lax.broadcasted_iota(jnp.int32, columns.shape, 1)
    ranks = jnp.sum(jnp.where(lanes == source, columns, 0), axis=1, keepdims=True)
    out = attend(got_ref[source, 0], ranks, rank_ref, key_scr, val_scr, score_scr)
    out_ref[0] = out.astype(BF16)


def attend_some(arrived, rank_columns, rank_row, first, count, after, earlier=None):
    heads, _, each, _ = arrived.shape
    total = heads * each
    specs = [
        vmem(),
        vmem(),
        vmem(),
        anywhere(),
    ]
    operands = [arrived, rank_columns, rank_row, after]
    aliases = {}
    if earlier is not None:
        specs.append(anywhere())
        operands.append(earlier)
        aliases = {len(operands) - 1: 0}
    return pl.pallas_call(
        functools.partial(attend_kernel, first),
        grid=(count,),
        in_specs=specs,
        out_specs=pl.BlockSpec((1, each, HD), lambda i: (i + first, 0, 0)),
        out_shape=jax.ShapeDtypeStruct((heads, each, HD), BF16),
        scratch_shapes=[
            pltpu.VMEM((total, HD), BF16),
            pltpu.VMEM((total, 2 * HD), BF16),
            pltpu.VMEM((each, total), F32),
        ],
        input_output_aliases=aliases,
        compiler_params=params(),
        name="attention",
    )(*operands)


def head_kernel(
    cond_ref, gain_ref, out_t_ref, noise_ref, feat_ref, base_hbm, after_ref,
    send_ref, token_ref, block_scr, base_ref, sem,
):
    fetch = pltpu.make_async_copy(base_hbm, base_ref, sem)
    fetch.start()
    heads, rows, width = cond_ref.shape
    count = base_ref.shape[0]
    condition = cond_ref[0].astype(F32)
    for source in range(1, heads):
        condition = condition + cond_ref[source].astype(F32)
    fetch.wait()
    hidden = base_ref[...] + jnp.concatenate([condition] * (count // rows), axis=0)
    inverse = lax.rsqrt(jnp.mean(hidden * hidden, axis=1, keepdims=True) + NORM_EPS)
    unit = hidden * inverse
    gain = gain_ref[...]
    scaled = unit * gain
    gate = 1.0 / (1.0 + jnp.exp(-scaled))
    active = scaled * gate
    act_hi, act_lo = two_parts(active)
    out_hi, out_lo = two_parts(out_t_ref[...])
    both = dot_rows(jnp.concatenate([act_hi, act_lo], axis=0), out_hi)
    predicted = both[:count] + both[count:] + dot_rows(act_hi, out_lo)
    pred_grad = (predicted - noise_ref[:, :LAT]) * noise_ref[:, LAT : LAT + 1]
    pg_hi, pg_lo = two_parts(pred_grad)
    both = dot(jnp.concatenate([pg_hi, pg_lo], axis=0), out_hi)
    act_grad = both[:count] + both[count:] + dot(pg_hi, out_lo)
    scaled_grad = act_grad * gate * (1.0 + scaled * (1.0 - gate))
    gain_grad = jnp.sum(scaled_grad * unit, axis=0, keepdims=True)
    unit_grad = scaled_grad * gain
    along = jnp.mean(unit_grad * unit, axis=1, keepdims=True)
    hidden_grad = inverse * (unit_grad - unit * along)
    hg_hi, hg_lo = two_parts(hidden_grad)
    feats = feat_ref[...]
    half = feats.shape[0] // 2
    both = dot(feats, hg_hi)
    feat_grad = both[:half] + both[half:] + dot(feats[:half], hg_lo)
    out_grad = dot_over_rows(pg_hi, act_hi) + dot_over_rows(pg_lo, act_hi)
    out_grad = out_grad + dot_over_rows(pg_hi, act_lo)
    token_ref[...] = inverse[:8] + jnp.zeros(token_ref.shape, F32)
    cond_grad = hidden_grad[:rows]
    for draw in range(1, count // rows):
        cond_grad = cond_grad + hidden_grad[draw * rows : (draw + 1) * rows]
    block_scr[:, :width] = cond_grad
    block_scr[:, width:] = jnp.zeros((rows, EXTRA), F32)
    pieces = width // EXTRA
    for target in range(heads):
        source_rows = feat_grad if 2 * target < LAT else out_grad
        begin = 2 * target % LAT
        block_scr[rows - 2 : rows, :width] = source_rows[begin : begin + 2]
        if target < pieces:
            cols = slice(target * EXTRA, (target + 1) * EXTRA)
            block_scr[0:1, width:] = feat_grad[LAT : LAT + 1, cols]
            block_scr[1:2, width:] = gain_grad[:, cols]
        elif target == pieces:
            block_scr[:, width:] = jnp.zeros((rows, EXTRA), F32)
        send_ref[target] = block_scr[...].astype(BF16)


def grad_kernel(got_ref, picked_ref, after_ref, send_ref, token_ref, pack_scr):
    heads, rows, wide = got_ref.shape
    width = wide - EXTRA
    groups = send_ref.shape[0]
    cond_grad = got_ref[:, :, :width].reshape(heads * rows, width)
    part = lax.dot_general(
        picked_ref[...], cond_grad, (((0,), (0,)), ((), ())), preferred_element_type=F32
    ).astype(BF16)
    summed = got_ref[0].astype(F32)
    for source in range(1, heads):
        summed = summed + got_ref[source].astype(F32)
    pack_scr[...] = jnp.zeros(pack_scr.shape, F32)
    pieces = width // 128
    for piece in range(pieces):
        row, lane = 2 * (piece % 8), 128 * (piece // 8)
        pack_scr[row : row + 2, lane : lane + 128] = summed[
            rows - 2 : rows, piece * 128 : (piece + 1) * 128
        ]
    row, lane = 2 * (pieces % 8), 128 * (pieces // 8)
    pack_scr[row : row + 2, lane : lane + 128] = summed[0:2, width:]
    packed = pack_scr[...].astype(BF16)
    token_ref[...] = summed[:8, :HD]
    row_groups = HD // GROUP_ROWS
    col_groups = groups // row_groups
    cols = width // col_groups
    for group in range(groups):
        top = group // col_groups * GROUP_ROWS
        left = group % col_groups * cols
        send_ref[group, :, :cols] = part[top : top + GROUP_ROWS, left : left + cols]
        send_ref[group, :, cols:] = packed


def total_kernel(got_ref, big_ref, tail_ref, token_ref):
    groups, rows, wide = got_ref.shape
    cols = wide - PACK
    total = got_ref[0].astype(F32)
    for source in range(1, groups):
        total = total + got_ref[source].astype(F32)
    token_ref[...] = total[:8, :HD]
    rounded = total.astype(BF16)
    for group in range(groups):
        big_ref[group] = rounded[:, :cols]
    for head in range(tail_ref.shape[0]):
        tail_ref[head, :rows] = rounded[:, cols : cols + HD]
        tail_ref[head, rows:] = rounded[:, cols + HD :]


def route_kernel(steps, place_ref, own_ref, other_ref, *rest):
    chips = other_ref.shape[0]
    for step, out_ref in zip(steps, rest[-len(steps) :]):
        target = lax.rem(place_ref[0] + step, chips)
        out_ref[0] = own_ref[2 * target + place_ref[1]]
        out_ref[1] = other_ref[target]


def collect_kernel(place_ref, *refs):
    out_ref = refs[-1]
    chips = len(refs) - 1
    for step in range(chips):
        source = lax.rem(place_ref[0] - step + chips, chips)
        for part in range(2):
            core = place_ref[1] if part == 0 else 1 - place_ref[1]
            left = pl.multiple_of((2 * source + core) * HD, HD)
            out_ref[:, pl.ds(left, HD)] = refs[step][part]


def smem():
    return pl.BlockSpec(memory_space=pltpu.SMEM)


def route(steps, place, own, other, after):
    _, each, _ = own.shape
    return pl.pallas_call(
        functools.partial(route_kernel, steps),
        in_specs=[smem(), vmem(), vmem(), anywhere()],
        out_specs=[vmem()] * len(steps),
        out_shape=[jax.ShapeDtypeStruct((2, each, HD), BF16)] * len(steps),
        compiler_params=params(),
        name="route",
    )(place, own, other, after)


def round_chips(value, step, heads):
    pairs = [(source, (source + 2 * step) % heads) for source in range(heads)]
    return lax.ppermute(value, "head", pairs)


def collect(place, pieces):
    _, each, _ = pieces[0].shape
    return pl.pallas_call(
        collect_kernel,
        in_specs=[smem()] + [vmem()] * len(pieces),
        out_specs=vmem(),
        out_shape=jax.ShapeDtypeStruct((each, 2 * len(pieces) * HD), BF16),
        compiler_params=params(),
        name="collect",
    )(place, *pieces)


def spread_kernel(big_ref, tail_ref, cond_ref, in_ref, time_ref, gain_ref, out_ref):
    groups, rows, cols = big_ref.shape
    heads = tail_ref.shape[0]
    width = cond_ref.shape[1]
    col_groups = width // cols
    for group in range(groups):
        top = group // col_groups * GROUP_ROWS
        left = group % col_groups * cols
        cond_ref[top : top + GROUP_ROWS, left : left + cols] = big_ref[group].astype(F32)
    pieces = width // 128
    for head in range(heads):
        packed = tail_ref[head].astype(F32)
        target = in_ref if 2 * head < LAT else out_ref
        begin = 2 * head % LAT
        for piece in range(pieces):
            row = 2 * (piece % 8) + GROUP_ROWS * (piece // 8)
            target[begin : begin + 2, piece * 128 : (piece + 1) * 128] = packed[row : row + 2]
        if head < pieces:
            row = 2 * (pieces % 8) + GROUP_ROWS * (pieces // 8)
            cut = slice(head * 128, (head + 1) * 128)
            time_ref[cut] = packed[row]
            gain_ref[cut] = packed[row + 1]


def call(kernel, out_shape, scratch, name, *operands, outside=0):
    specs = [vmem()] * (len(operands) - outside) + [anywhere()] * outside
    many = isinstance(out_shape, list)
    return pl.pallas_call(
        kernel,
        in_specs=specs,
        out_specs=[vmem()] * len(out_shape) if many else vmem(),
        out_shape=out_shape,
        scratch_shapes=scratch,
        compiler_params=params(),
        name=name,
    )(*operands)


def exchange(value, axis):
    return lax.all_to_all(value, axis, split_axis=0, concat_axis=0, tiled=True)


def local(
    queries, key_rows, value_rows, token_rank, masked_index, masked_counts, clean_latents,
    noise_draws, noise_times, w_cond, w_in, time_vec, norm_gain, w_out,
):
    each = queries.shape[0]
    heads = lax.axis_size("head")
    groups = lax.axis_size("seq")
    total = each * heads
    width = w_cond.shape[1]
    share = masked_index.shape[1] // heads
    count = DRAWS * SLOT

    stacked = stack_by_head(queries, key_rows, value_rows, heads)
    arrived = in_vmem(exchange(stacked, "head"))

    chosen = masked_index[0]
    live = lax.dynamic_index_in_dim(masked_counts, lax.axis_index("seq"), 0, keepdims=False)
    alive = jnp.arange(heads * share, dtype=jnp.int32) < live
    ranks = token_rank[0]

    def in_slots(value, fill):
        value = value.reshape(heads, share)
        return jnp.pad(value, ((0, 0), (0, SLOT - share)), constant_values=fill)

    where = in_slots(jnp.where(alive, chosen, -1), -1).reshape(heads * SLOT)
    where_rank = in_slots(jnp.where(alive, jnp.take(ranks, chosen), -1), -1)
    slot_columns = jnp.stack([where, where_rank.reshape(heads * SLOT)], axis=1)
    rank_row = ranks.reshape(1, total)
    rank_columns = jnp.pad(ranks.reshape(heads, each).T, ((0, 0), (0, 128 - heads)))

    mine = lax.dynamic_index_in_dim(
        in_slots(chosen, 0), lax.axis_index("head"), 0, keepdims=False
    )
    my_alive = lax.dynamic_index_in_dim(
        in_slots(alive.astype(F32), 0.0), lax.axis_index("head"), 0, keepdims=False
    )
    clean = jnp.take(clean_latents, mine, axis=0).astype(F32)
    noise = jnp.take(noise_draws, mine, axis=0).astype(F32)
    times = jnp.take(noise_times, mine, axis=0).astype(F32)
    noise = jnp.transpose(noise.reshape(SLOT, DRAWS, LAT), (1, 0, 2))
    times = jnp.transpose(times)[:, :, None]
    angles = 0.5 * math.pi * times
    noisy = (jnp.cos(angles) * clean[None] + jnp.sin(angles) * noise).reshape(count, LAT)
    times = times.reshape(count, 1)
    noise = noise.reshape(count, LAT)
    base = jnp.dot(noisy, w_in, precision=lax.Precision.HIGHEST) + times * time_vec
    loss_scale = 1.0 / math.sqrt(masked_index.shape[1] // 3 * groups * DRAWS)
    row_weight = jnp.tile(my_alive * (2.0 * loss_scale), DRAWS).reshape(count, 1)
    feats = jnp.pad(jnp.concatenate([noisy, times], axis=1), ((0, 0), (0, 15))).T
    feats = jnp.concatenate(two_parts(feats), axis=0)

    gain = norm_gain.reshape(1, width)
    noise = jnp.concatenate([noise, row_weight], axis=1)
    slot_columns, rank_columns, base, gain, noise, feats = lax.optimization_barrier(
        (slot_columns, rank_columns, base, gain, noise, feats)
    )
    part, picked = attend_masked(arrived, slot_columns, rank_row, w_cond)
    half = heads // 2
    got_cond = exchange(part, "head")
    first_half = attend_some(arrived, rank_columns, rank_row, 0, half, picked)

    send, token = call(
        head_kernel,
        [
            pltpu.HBM((heads, SLOT, width + EXTRA), BF16),
            jax.ShapeDtypeStruct((8, 128), F32),
        ],
        [
            pltpu.VMEM((SLOT, width + EXTRA), F32),
            pltpu.VMEM(base.shape, F32),
            pltpu.SemaphoreType.DMA,
        ],
        "diffusion_head",
        in_vmem(got_cond), gain, w_out.T, noise, feats, in_hbm(base), first_half,
        outside=2,
    )
    got_grad = exchange(send, "head")
    attended = attend_some(arrived, rank_columns, rank_row, half, half, token, first_half)

    col_groups = groups // (HD // GROUP_ROWS)
    cols = width // col_groups
    place = lax.axis_index("head")
    core = lax.rem(place, 2)
    place = jnp.stack([place // 2, core])
    to_other = lax.dynamic_index_in_dim(
        attended.reshape(half, 2, each, HD), 1 - core, 1, keepdims=False
    )
    other = lax.ppermute(to_other, "head", [(i, i ^ 1) for i in range(heads)])
    parts, token = call(
        grad_kernel,
        [
            jax.ShapeDtypeStruct((groups, GROUP_ROWS, cols + PACK), BF16),
            jax.ShapeDtypeStruct((8, HD), F32),
        ],
        [pltpu.VMEM((GROUP_ROWS, PACK), F32)],
        "cond_weight_grad",
        in_vmem(got_grad), picked, attended,
        outside=1,
    )
    got_parts = exchange(parts, "seq")
    early, late = tuple(range(EARLY)), tuple(range(EARLY, half))
    messages = route(early, place, attended, other, token)
    pieces = [messages[0]] + [round_chips(messages[k], k, heads) for k in early[1:]]
    big, small, token = call(
        total_kernel,
        [
            jax.ShapeDtypeStruct((groups, GROUP_ROWS, cols), BF16),
            jax.ShapeDtypeStruct((heads, TAIL, HD), BF16),
            jax.ShapeDtypeStruct((8, HD), F32),
        ],
        [],
        "sum_over_clips",
        in_vmem(got_parts),
    )
    all_big = exchange(big, "seq")
    messages = route(late, place, attended, other, token)
    pieces += [round_chips(message, k, heads) for k, message in zip(late, messages)]
    all_small = exchange(small, "head")
    cond_whole, in_grad, time_grad, gain_grad, out_grad = call(
        spread_kernel,
        [
            jax.ShapeDtypeStruct((HD, width), F32),
            jax.ShapeDtypeStruct((LAT, width), F32),
            jax.ShapeDtypeStruct((width,), F32),
            jax.ShapeDtypeStruct((width,), F32),
            jax.ShapeDtypeStruct((LAT, width), F32),
        ],
        [],
        "write_gradients",
        in_vmem(all_big), in_vmem(all_small),
    )
    rows = collect(place, pieces)
    return (rows, cond_whole, in_grad, time_grad, gain_grad, out_grad.T)


def solution(mesh):
    return jax.shard_map(
        local,
        mesh=mesh,
        in_specs=(
            P(("seq", "head"), None),
            P(("seq", "head"), None),
            P(("seq", "head"), None),
            P("seq", None),
            P("seq", None),
            P(),
            P("seq", None),
            P("seq", None),
            P("seq", None),
            P("head", None),
            P(),
            P(),
            P(),
            P(),
        ),
        out_specs=(P(("seq", "head"), None), P("head", None), P(), P(), P(), P()),
        check_vma=False,
    )
```

```python
import functools
import math

import jax
import jax.numpy as jnp
from jax import lax
from jax.experimental import pallas as pl
from jax.experimental.pallas import tpu as pltpu
from jax.sharding import PartitionSpec as P

HD = 128
LAT = 16
DRAWS = 4
NORM_EPS = 1e-06
HIDDEN_SCORE = -1e30
SLOT = 16
EARLY = 5
EXTRA = 128
PACK = 256
TAIL = 32
GROUP_ROWS = 16
LOG2E = 1.4426950408889634
F32 = jnp.float32
BF16 = jnp.bfloat16
VMEM_LIMIT = 32 * 1024 * 1024


def params():
    return pltpu.CompilerParams(vmem_limit_bytes=VMEM_LIMIT)


def vmem():
    return pl.BlockSpec(memory_space=pltpu.VMEM)


def anywhere():
    return pl.BlockSpec(memory_space=pl.ANY)


def dot(a, b):
    return jnp.dot(a, b, preferred_element_type=F32)


def dot_rows(a, b):
    return lax.dot_general(a, b, (((1,), (1,)), ((), ())), preferred_element_type=F32)


def dot_over_rows(a, b):
    return lax.dot_general(a, b, (((0,), (0,)), ((), ())), preferred_element_type=F32)


def two_parts(value):
    high = value.astype(BF16)
    return high, (value - high.astype(F32)).astype(BF16)


def in_vmem(value):
    return pltpu.with_memory_space_constraint(value, pltpu.VMEM)


def in_hbm(value):
    return pltpu.with_memory_space_constraint(value, pltpu.HBM)


def stack_kernel(q_ref, k_ref, v_ref, out_ref):
    for head in range(out_ref.shape[0]):
        cols = slice(head * HD, (head + 1) * HD)
        out_ref[head, 0] = q_ref[:, cols]
        out_ref[head, 1] = k_ref[:, cols]
        out_ref[head, 2] = v_ref[:, cols]


def stack_by_head(queries, key_rows, value_rows, heads):
    each = queries.shape[0]
    block = each // 2
    spec = pl.BlockSpec((block, heads * HD), lambda i: (i, 0))
    return pl.pallas_call(
        stack_kernel,
        grid=(2,),
        in_specs=[spec, spec, spec],
        out_specs=pl.BlockSpec((heads, 3, block, HD), lambda i: (0, 0, i, 0)),
        out_shape=pltpu.HBM((heads, 3, each, HD), BF16),
        compiler_params=params(),
        name="stack_by_head",
    )(in_hbm(queries), in_hbm(key_rows), in_hbm(value_rows))


def load_keys(got_ref, key_scr, val_scr):
    rows = key_scr.shape[0]
    key_scr[...] = got_ref[:, 1].reshape(rows, HD)
    val_scr[:, :HD] = got_ref[:, 2].reshape(rows, HD)
    val_scr[:, HD:] = jnp.ones((rows, HD), BF16)


def attend(query, query_rank, rank_ref, key_scr, val_scr, score_scr):
    total = key_scr.shape[0]
    chunk = math.gcd(total, 512)
    scale = LOG2E / math.sqrt(HD)
    top = None
    for start in range(0, total, chunk):
        scores = lax.dot_general(
            query,
            key_scr[start : start + chunk, :],
            (((1,), (1,)), ((), ())),
            preferred_element_type=F32,
        )
        visible = rank_ref[:, start : start + chunk] <= query_rank
        scores = jnp.where(visible, scores, HIDDEN_SCORE)
        score_scr[:, start : start + chunk] = scores
        for lane in range(0, chunk, 128):
            part = scores[:, lane : lane + 128]
            top = part if top is None else jnp.maximum(top, part)
    top = jnp.max(top, axis=1, keepdims=True)
    total_out = None
    for start in range(0, total, chunk):
        weights = jnp.exp2((score_scr[:, start : start + chunk] - top) * scale)
        mixed = dot(weights.astype(BF16), val_scr[start : start + chunk, :])
        total_out = mixed if total_out is None else total_out + mixed
    return total_out[:, :HD] / total_out[:, HD:]


def masked_kernel(got_ref, slot_ref, rank_ref, w_ref, *rest):
    part_ref, picked_ref, key_scr, val_scr, score_scr, w_scr, sem = rest
    fetch = pltpu.make_async_copy(w_ref, w_scr, sem)
    fetch.start()
    load_keys(got_ref, key_scr, val_scr)
    slots = slot_ref.shape[0]
    where = slot_ref[:, 0:1]
    slot_rank = slot_ref[:, 1:2]
    total = key_scr.shape[0]
    sources, _, each, _ = got_ref.shape
    query = jnp.zeros((slots, HD), F32)
    step = math.gcd(each * sources, each * 4)
    for start in range(0, total, step):
        lanes = lax.broadcasted_iota(jnp.int32, (slots, step), 1) + start
        hit = jnp.where(lanes == where, 1.0, 0.0).astype(BF16)
        rows = got_ref[start // each : (start + step) // each, 0].reshape(step, HD)
        query = query + dot(hit, rows)
    out = attend(query.astype(BF16), slot_rank, rank_ref, key_scr, val_scr, score_scr)
    picked = jnp.where(slot_rank >= 0, out, 0.0).astype(BF16)
    picked_ref[...] = picked
    fetch.wait()
    part = dot(picked, w_scr[...]).astype(BF16)
    part_ref[...] = part.reshape(part_ref.shape)


def attend_masked(arrived, slot_columns, rank_row, w_cond):
    heads, _, each, _ = arrived.shape
    total = heads * each
    slots = slot_columns.shape[0]
    width = w_cond.shape[1]
    return pl.pallas_call(
        masked_kernel,
        in_specs=[vmem()] * 3 + [anywhere()],
        out_specs=[vmem(), vmem()],
        out_shape=[
            pltpu.HBM((heads, slots // heads, width), BF16),
            jax.ShapeDtypeStruct((slots, HD), BF16),
        ],
        scratch_shapes=[
            pltpu.VMEM((total, HD), BF16),
            pltpu.VMEM((total, 2 * HD), BF16),
            pltpu.VMEM((slots, total), F32),
            pltpu.VMEM(w_cond.shape, BF16),
            pltpu.SemaphoreType.DMA,
        ],
        compiler_params=params(),
        name="masked_rows",
    )(arrived, slot_columns, rank_row, in_hbm(w_cond))


def attend_kernel(first, got_ref, qrank_ref, rank_ref, *rest):
    out_ref, key_scr, val_scr, score_scr = rest[-4:]

    @pl.when(pl.program_id(0) == 0)
    def _():
        load_keys(got_ref, key_scr, val_scr)

    source = pl.program_id(0) + first
    columns = qrank_ref[...]
    lanes = lax.broadcasted_iota(jnp.int32, columns.shape, 1)
    ranks = jnp.sum(jnp.where(lanes == source, columns, 0), axis=1, keepdims=True)
    out = attend(got_ref[source, 0], ranks, rank_ref, key_scr, val_scr, score_scr)
    out_ref[0] = out.astype(BF16)


def attend_some(arrived, rank_columns, rank_row, first, count, after, earlier=None):
    heads, _, each, _ = arrived.shape
    total = heads * each
    specs = [
        vmem(),
        vmem(),
        vmem(),
        anywhere(),
    ]
    operands = [arrived, rank_columns, rank_row, after]
    aliases = {}
    if earlier is not None:
        specs.append(anywhere())
        operands.append(in_hbm(earlier))
        aliases = {len(operands) - 1: 0}
    return pl.pallas_call(
        functools.partial(attend_kernel, first),
        grid=(count,),
        in_specs=specs,
        out_specs=pl.BlockSpec((1, each, HD), lambda i: (i + first, 0, 0)),
        out_shape=pltpu.HBM((heads, each, HD), BF16),
        scratch_shapes=[
            pltpu.VMEM((total, HD), BF16),
            pltpu.VMEM((total, 2 * HD), BF16),
            pltpu.VMEM((each, total), F32),
        ],
        input_output_aliases=aliases,
        compiler_params=params(),
        name="attention",
    )(*operands)


def head_kernel(
    cond_ref, gain_ref, out_t_ref, noise_ref, feat_ref, base_hbm, after_ref,
    send_ref, token_ref, block_scr, base_ref, sem,
):
    fetch = pltpu.make_async_copy(base_hbm, base_ref, sem)
    fetch.start()
    heads, rows, width = cond_ref.shape
    count = base_ref.shape[0]
    condition = cond_ref[0].astype(F32)
    for source in range(1, heads):
        condition = condition + cond_ref[source].astype(F32)
    fetch.wait()
    hidden = base_ref[...] + jnp.concatenate([condition] * (count // rows), axis=0)
    inverse = lax.rsqrt(jnp.mean(hidden * hidden, axis=1, keepdims=True) + NORM_EPS)
    unit = hidden * inverse
    gain = gain_ref[...]
    scaled = unit * gain
    gate = 1.0 / (1.0 + jnp.exp(-scaled))
    active = scaled * gate
    act_hi, act_lo = two_parts(active)
    out_hi, out_lo = two_parts(out_t_ref[...])
    both = dot_rows(jnp.concatenate([act_hi, act_lo], axis=0), out_hi)
    predicted = both[:count] + both[count:] + dot_rows(act_hi, out_lo)
    pred_grad = (predicted - noise_ref[:, :LAT]) * noise_ref[:, LAT : LAT + 1]
    pg_hi, pg_lo = two_parts(pred_grad)
    both = dot(jnp.concatenate([pg_hi, pg_lo], axis=0), out_hi)
    act_grad = both[:count] + both[count:] + dot(pg_hi, out_lo)
    scaled_grad = act_grad * gate * (1.0 + scaled * (1.0 - gate))
    gain_grad = jnp.sum(scaled_grad * unit, axis=0, keepdims=True)
    unit_grad = scaled_grad * gain
    along = jnp.mean(unit_grad * unit, axis=1, keepdims=True)
    hidden_grad = inverse * (unit_grad - unit * along)
    hg_hi, hg_lo = two_parts(hidden_grad)
    feats = feat_ref[...]
    half = feats.shape[0] // 2
    both = dot(feats, hg_hi)
    feat_grad = both[:half] + both[half:] + dot(feats[:half], hg_lo)
    out_grad = dot_over_rows(pg_hi, act_hi) + dot_over_rows(pg_lo, act_hi)
    out_grad = out_grad + dot_over_rows(pg_hi, act_lo)
    token_ref[...] = inverse[:8] + jnp.zeros(token_ref.shape, F32)
    cond_grad = hidden_grad[:rows]
    for draw in range(1, count // rows):
        cond_grad = cond_grad + hidden_grad[draw * rows : (draw + 1) * rows]
    block_scr[:, :width] = cond_grad
    block_scr[:, width:] = jnp.zeros((rows, EXTRA), F32)
    pieces = width // EXTRA
    for target in range(heads):
        source_rows = feat_grad if 2 * target < LAT else out_grad
        begin = 2 * target % LAT
        block_scr[rows - 2 : rows, :width] = source_rows[begin : begin + 2]
        if target < pieces:
            cols = slice(target * EXTRA, (target + 1) * EXTRA)
            block_scr[0:1, width:] = feat_grad[LAT : LAT + 1, cols]
            block_scr[1:2, width:] = gain_grad[:, cols]
        elif target == pieces:
            block_scr[:, width:] = jnp.zeros((rows, EXTRA), F32)
        send_ref[target] = block_scr[...].astype(BF16)


def grad_kernel(got_ref, picked_ref, after_ref, send_ref, token_ref, pack_scr):
    heads, rows, wide = got_ref.shape
    width = wide - EXTRA
    groups = send_ref.shape[0]
    cond_grad = got_ref[:, :, :width].reshape(heads * rows, width)
    part = lax.dot_general(
        picked_ref[...], cond_grad, (((0,), (0,)), ((), ())), preferred_element_type=F32
    ).astype(BF16)
    summed = got_ref[0].astype(F32)
    for source in range(1, heads):
        summed = summed + got_ref[source].astype(F32)
    pack_scr[...] = jnp.zeros(pack_scr.shape, F32)
    pieces = width // 128
    for piece in range(pieces):
        row, lane = 2 * (piece % 8), 128 * (piece // 8)
        pack_scr[row : row + 2, lane : lane + 128] = summed[
            rows - 2 : rows, piece * 128 : (piece + 1) * 128
        ]
    row, lane = 2 * (pieces % 8), 128 * (pieces // 8)
    pack_scr[row : row + 2, lane : lane + 128] = summed[0:2, width:]
    packed = pack_scr[...].astype(BF16)
    token_ref[...] = summed[:8, :HD]
    row_groups = HD // GROUP_ROWS
    col_groups = groups // row_groups
    cols = width // col_groups
    for group in range(groups):
        top = group // col_groups * GROUP_ROWS
        left = group % col_groups * cols
        send_ref[group, :, :cols] = part[top : top + GROUP_ROWS, left : left + cols]
        send_ref[group, :, cols:] = packed


def total_kernel(got_ref, big_ref, tail_ref, token_ref):
    groups, rows, wide = got_ref.shape
    cols = wide - PACK
    total = got_ref[0].astype(F32)
    for source in range(1, groups):
        total = total + got_ref[source].astype(F32)
    token_ref[...] = total[:8, :HD]
    rounded = total.astype(BF16)
    for group in range(groups):
        big_ref[group] = rounded[:, :cols]
    for head in range(tail_ref.shape[0]):
        tail_ref[head, :rows] = rounded[:, cols : cols + HD]
        tail_ref[head, rows:] = rounded[:, cols + HD :]


def route_kernel(steps, place_ref, own_ref, other_ref, *rest):
    chips = other_ref.shape[0]
    for step, out_ref in zip(steps, rest[-len(steps) :]):
        target = lax.rem(place_ref[0] + step, chips)
        out_ref[0] = own_ref[2 * target + place_ref[1]]
        out_ref[1] = other_ref[target]


def collect_kernel(place_ref, *refs):
    out_ref = refs[-1]
    chips = len(refs) - 1
    for step in range(chips):
        source = lax.rem(place_ref[0] - step + chips, chips)
        for part in range(2):
            core = place_ref[1] if part == 0 else 1 - place_ref[1]
            left = pl.multiple_of((2 * source + core) * HD, HD)
            out_ref[:, pl.ds(left, HD)] = refs[step][part]


def smem():
    return pl.BlockSpec(memory_space=pltpu.SMEM)


def route(steps, place, own, other, after):
    _, each, _ = own.shape
    return pl.pallas_call(
        functools.partial(route_kernel, steps),
        in_specs=[smem(), vmem(), vmem(), anywhere()],
        out_specs=[vmem()] * len(steps),
        out_shape=[jax.ShapeDtypeStruct((2, each, HD), BF16)] * len(steps),
        compiler_params=params(),
        name="route",
    )(place, in_hbm(own), other, after)


def round_chips(value, step, heads):
    pairs = [(source, (source + 2 * step) % heads) for source in range(heads)]
    return lax.ppermute(value, "head", pairs)


def collect(place, pieces):
    _, each, _ = pieces[0].shape
    return pl.pallas_call(
        collect_kernel,
        in_specs=[smem()] + [vmem()] * len(pieces),
        out_specs=vmem(),
        out_shape=jax.ShapeDtypeStruct((each, 2 * len(pieces) * HD), BF16),
        compiler_params=params(),
        name="collect",
    )(place, *pieces)


def spread_kernel(big_ref, tail_ref, cond_ref, in_ref, time_ref, gain_ref, out_ref):
    groups, rows, cols = big_ref.shape
    heads = tail_ref.shape[0]
    width = cond_ref.shape[1]
    col_groups = width // cols
    for group in range(groups):
        top = group // col_groups * GROUP_ROWS
        left = group % col_groups * cols
        cond_ref[top : top + GROUP_ROWS, left : left + cols] = big_ref[group].astype(F32)
    pieces = width // 128
    for head in range(heads):
        packed = tail_ref[head].astype(F32)
        target = in_ref if 2 * head < LAT else out_ref
        begin = 2 * head % LAT
        for piece in range(pieces):
            row = 2 * (piece % 8) + GROUP_ROWS * (piece // 8)
            target[begin : begin + 2, piece * 128 : (piece + 1) * 128] = packed[row : row + 2]
        if head < pieces:
            row = 2 * (pieces % 8) + GROUP_ROWS * (pieces // 8)
            cut = slice(head * 128, (head + 1) * 128)
            time_ref[cut] = packed[row]
            gain_ref[cut] = packed[row + 1]


def call(kernel, out_shape, scratch, name, *operands, outside=0):
    specs = [vmem()] * (len(operands) - outside) + [anywhere()] * outside
    many = isinstance(out_shape, list)
    return pl.pallas_call(
        kernel,
        in_specs=specs,
        out_specs=[vmem()] * len(out_shape) if many else vmem(),
        out_shape=out_shape,
        scratch_shapes=scratch,
        compiler_params=params(),
        name=name,
    )(*operands)


def exchange(value, axis):
    return lax.all_to_all(value, axis, split_axis=0, concat_axis=0, tiled=True)


def local(
    queries, key_rows, value_rows, token_rank, masked_index, masked_counts, clean_latents,
    noise_draws, noise_times, w_cond, w_in, time_vec, norm_gain, w_out,
):
    each = queries.shape[0]
    heads = lax.axis_size("head")
    groups = lax.axis_size("seq")
    total = each * heads
    width = w_cond.shape[1]
    share = masked_index.shape[1] // heads
    count = DRAWS * SLOT

    stacked = stack_by_head(queries, key_rows, value_rows, heads)
    arrived = in_vmem(exchange(stacked, "head"))

    chosen = masked_index[0]
    live = lax.dynamic_index_in_dim(masked_counts, lax.axis_index("seq"), 0, keepdims=False)
    alive = jnp.arange(heads * share, dtype=jnp.int32) < live
    ranks = token_rank[0]

    def in_slots(value, fill):
        value = value.reshape(heads, share)
        return jnp.pad(value, ((0, 0), (0, SLOT - share)), constant_values=fill)

    where = in_slots(jnp.where(alive, chosen, -1), -1).reshape(heads * SLOT)
    where_rank = in_slots(jnp.where(alive, jnp.take(ranks, chosen), -1), -1)
    slot_columns = jnp.stack([where, where_rank.reshape(heads * SLOT)], axis=1)
    rank_row = ranks.reshape(1, total)
    rank_columns = jnp.pad(ranks.reshape(heads, each).T, ((0, 0), (0, 128 - heads)))

    mine = lax.dynamic_index_in_dim(
        in_slots(chosen, 0), lax.axis_index("head"), 0, keepdims=False
    )
    my_alive = lax.dynamic_index_in_dim(
        in_slots(alive.astype(F32), 0.0), lax.axis_index("head"), 0, keepdims=False
    )
    clean = jnp.take(clean_latents, mine, axis=0).astype(F32)
    noise = jnp.take(noise_draws, mine, axis=0).astype(F32)
    times = jnp.take(noise_times, mine, axis=0).astype(F32)
    noise = jnp.transpose(noise.reshape(SLOT, DRAWS, LAT), (1, 0, 2))
    times = jnp.transpose(times)[:, :, None]
    angles = 0.5 * math.pi * times
    noisy = (jnp.cos(angles) * clean[None] + jnp.sin(angles) * noise).reshape(count, LAT)
    times = times.reshape(count, 1)
    noise = noise.reshape(count, LAT)
    base = jnp.dot(noisy, w_in, precision=lax.Precision.HIGHEST) + times * time_vec
    loss_scale = 1.0 / math.sqrt(masked_index.shape[1] // 3 * groups * DRAWS)
    row_weight = jnp.tile(my_alive * (2.0 * loss_scale), DRAWS).reshape(count, 1)
    feats = jnp.pad(jnp.concatenate([noisy, times], axis=1), ((0, 0), (0, 15))).T
    feats = jnp.concatenate(two_parts(feats), axis=0)

    gain = norm_gain.reshape(1, width)
    noise = jnp.concatenate([noise, row_weight], axis=1)
    slot_columns, rank_columns, base, gain, noise, feats = lax.optimization_barrier(
        (slot_columns, rank_columns, base, gain, noise, feats)
    )
    part, picked = attend_masked(arrived, slot_columns, rank_row, w_cond)
    half = heads // 2
    got_cond = exchange(part, "head")
    first_half = attend_some(arrived, rank_columns, rank_row, 0, half, picked)

    send, token = call(
        head_kernel,
        [
            pltpu.HBM((heads, SLOT, width + EXTRA), BF16),
            jax.ShapeDtypeStruct((8, 128), F32),
        ],
        [
            pltpu.VMEM((SLOT, width + EXTRA), F32),
            pltpu.VMEM(base.shape, F32),
            pltpu.SemaphoreType.DMA,
        ],
        "diffusion_head",
        in_vmem(got_cond), gain, w_out.T, noise, feats, in_hbm(base), in_hbm(first_half),
        outside=2,
    )
    got_grad = exchange(send, "head")
    attended = attend_some(arrived, rank_columns, rank_row, half, half, token, first_half)

    col_groups = groups // (HD // GROUP_ROWS)
    cols = width // col_groups
    place = lax.axis_index("head")
    core = lax.rem(place, 2)
    place = jnp.stack([place // 2, core])
    to_other = lax.dynamic_index_in_dim(
        attended.reshape(half, 2, each, HD), 1 - core, 1, keepdims=False
    )
    other = lax.ppermute(to_other, "head", [(i, i ^ 1) for i in range(heads)])
    got_grad, other = lax.optimization_barrier((got_grad, other))
    parts, token = call(
        grad_kernel,
        [
            jax.ShapeDtypeStruct((groups, GROUP_ROWS, cols + PACK), BF16),
            jax.ShapeDtypeStruct((8, HD), F32),
        ],
        [pltpu.VMEM((GROUP_ROWS, PACK), F32)],
        "cond_weight_grad",
        in_vmem(got_grad), picked, token,
        outside=1,
    )
    got_parts = exchange(parts, "seq")
    early, late = tuple(range(EARLY)), tuple(range(EARLY, half))
    messages = route(early, place, attended, other, token)
    pieces = [messages[0]] + [round_chips(messages[k], k, heads) for k in early[1:]]
    got_parts, *pieces = lax.optimization_barrier((got_parts, *pieces))
    big, small, token = call(
        total_kernel,
        [
            jax.ShapeDtypeStruct((groups, GROUP_ROWS, cols), BF16),
            jax.ShapeDtypeStruct((heads, TAIL, HD), BF16),
            jax.ShapeDtypeStruct((8, HD), F32),
        ],
        [],
        "sum_over_clips",
        in_vmem(got_parts),
    )
    all_big = exchange(big, "seq")
    messages = route(late, place, attended, other, token)
    later = [round_chips(message, k, heads) for k, message in zip(late, messages)]
    all_big, small, *later = lax.optimization_barrier((all_big, small, *later))
    pieces = [*pieces, *later]
    all_small = exchange(small, "head")
    cond_whole, in_grad, time_grad, gain_grad, out_grad = call(
        spread_kernel,
        [
            jax.ShapeDtypeStruct((HD, width), F32),
            jax.ShapeDtypeStruct((LAT, width), F32),
            jax.ShapeDtypeStruct((width,), F32),
            jax.ShapeDtypeStruct((width,), F32),
            jax.ShapeDtypeStruct((LAT, width), F32),
        ],
        [],
        "write_gradients",
        in_vmem(all_big), in_vmem(all_small),
    )
    rows = collect(place, pieces)
    return (rows, cond_whole, in_grad, time_grad, gain_grad, out_grad.T)


def solution(mesh):
    return jax.shard_map(
        local,
        mesh=mesh,
        in_specs=(
            P(("seq", "head"), None),
            P(("seq", "head"), None),
            P(("seq", "head"), None),
            P("seq", None),
            P("seq", None),
            P(),
            P("seq", None),
            P("seq", None),
            P("seq", None),
            P("head", None),
            P(),
            P(),
            P(),
            P(),
        ),
        out_specs=(P(("seq", "head"), None), P("head", None), P(), P(), P(), P()),
        check_vma=False,
    )
```
